32 devices in a mesh: rad: 4 (over y, core), azi: 8 (over z, x).
Axes of the slice: x: 2, y: 2, z: 4, core: 2. Of those that a mesh axis runs over, the one named last changes fastest.
Arguments:
- fields: float32 [5, 8, 512, 512], P(None, None, 'azi', 'rad'), may hold values from -6 to 6
- radial_metric: float32 [512], P('rad'), may hold values from 0.5 to 2
- azimuth_metric: float32 [512], P('rad'), may hold values from 0.5 to 2
Outputs:
- grad_azimuth: float32 [5, 8, 512, 512], P(None, None, 'azi', 'rad')
- grad_radial: float32 [5, 8, 512, 512], P(None, None, 'azi', 'rad')
- filtered: float32 [5, 8, 512, 512], P(None, None, 'azi', 'rad')
The draws below stay inside these ranges and needn't reach their ends.
All inputs are finite; a program needn't handle non-finite values.
Results may differ from the reference program's by a relative error of at most 0.0003.
Values sent between devices are 32-bit elements; how exact they have to be, the bound alone decides.
A program may use at most 192 MiB of HBM per device.

```python
import math
import jax
import jax.numpy as jnp
from jax import lax

NF = 5
AX = 8
NT = 512
NR = 512


def levels(rng, extent, shards, smallest, top_value):
    def one(dim, blocks):
        heights = jax.random.uniform(jax.random.fold_in(jax.random.fold_in(rng, 6), dim), (blocks,), jnp.float32, smallest / len(shards), top_value / len(shards))
        return jnp.repeat(jnp.exp(heights), extent[dim] // blocks).reshape((-1,) + (1,) * (len(extent) - dim - 1))

    loudness = one(*shards[0])
    for cut in shards[1:]:
        loudness = loudness * one(*cut)
    return loudness


def normal_values(rng, shape, scale, bound, cuts=(), kind=jnp.bfloat16):
    values = jax.random.normal(rng, shape, jnp.float32) * scale
    if len(cuts) > 0:
        values = levels(rng, shape, cuts, -0.22, 0.18) * values
    return jnp.clip(values, min=-bound, max=bound).astype(kind)


def setup_inputs(seed: int = 0) -> dict:
    keys = jax.random.split(jax.random.key(seed), 4)
    return {
        "fields": normal_values(keys[0], (NF, AX, NT, NR), 1.0, 6.0, ((2, 8), (3, 4)), jnp.float32),
        "radial_metric": jnp.clip(jnp.exp(math.log(2.0) - 1.3862944 * jax.random.uniform(keys[1], (NR,), jnp.float32) ** levels(keys[1], (NR,), ((0, 4),), -0.2, 0.2)), 0.5, 2.0),
        "azimuth_metric": jnp.clip(jnp.exp(math.log(2.0) - 1.3862944 * jax.random.uniform(keys[2], (NR,), jnp.float32) ** levels(keys[2], (NR,), ((0, 4),), -0.2, 0.2)), 0.5, 2.0),
    }


ALPHA_D = 1.0 / 3.0
COEF_A = 14.0 / 9.0
COEF_B = 1.0 / 9.0
ALPHA_F = 0.49

def filter_weights():
    slack = 1.0 - 2.0 * ALPHA_F
    return [(193.0 + 126.0 * ALPHA_F) / 256.0, (105.0 + 302.0 * ALPHA_F) / 256.0, -15.0 * slack / 64.0, 45.0 * slack / 512.0, -5.0 * slack / 256.0, slack / 512.0]

def periodic_solve(source, alpha):
    count = source.shape[1]
    waves = jnp.arange(count).astype(source.dtype)
    symbol = 1.0 + 2.0 * alpha * jnp.cos(2.0 * jnp.pi * waves / count)
    spectrum = jnp.fft.fft(source, axis=1) / symbol[:, None]
    return jnp.real(jnp.fft.ifft(spectrum, axis=1)).astype(source.dtype)

def one_field(field):

    def along(offset):
        return jnp.roll(field, -offset, axis=1)
    slope_side = 0.5 * COEF_A * (along(1) - along(-1)) + 0.25 * COEF_B * (along(2) - along(-2))
    weights = filter_weights()
    smooth_side = weights[0] * field
    for offset in range(1, 6):
        smooth_side = smooth_side + 0.5 * weights[offset] * (along(offset) + along(-offset))
    slope_azi = periodic_solve(slope_side, ALPHA_D)
    smoothed = periodic_solve(smooth_side, ALPHA_F)
    count = field.shape[2]
    padded = jnp.pad(field, ((0, 0), (0, 0), (2, 2)))

    def radial(offset):
        return padded[:, :, 2 + offset:2 + offset + count]
    radial_side = 0.5 * COEF_A * (radial(1) - radial(-1)) + 0.25 * COEF_B * (radial(2) - radial(-2))
    flat = radial_side.reshape(-1, count).T
    lower = jnp.full((count,), ALPHA_D, field.dtype).at[0].set(0.0)
    upper = jnp.full((count,), ALPHA_D, field.dtype).at[count - 1].set(0.0)
    middle = jnp.ones((count,), field.dtype)
    solved = lax.linalg.tridiagonal_solve(lower, middle, upper, flat)
    slope_rad = solved.T.reshape(field.shape)
    return (slope_azi, slope_rad, smoothed)

def reference(fields, radial_metric, azimuth_metric):
    slope_azi, slope_rad, smoothed = lax.map(one_field, fields)
    return (slope_azi * azimuth_metric, slope_rad * radial_metric, smoothed)
```

```python
import functools

import jax
import jax.numpy as jnp
import ml_dtypes
import numpy as np
from jax import lax
from jax.experimental import pallas as pl
from jax.experimental.pallas import tpu as pltpu
from jax.sharding import PartitionSpec as P

ALPHA_D = 1.0 / 3.0
COEF_A = 14.0 / 9.0
COEF_B = 1.0 / 9.0
ALPHA_F = 0.49
MESH = pl.DeviceIdType.MESH
BF16 = jnp.bfloat16
F32 = jnp.float32

EDGE = 6
PACK = 4


def filter_weights():
    slack = 1.0 - 2.0 * ALPHA_F
    return [
        (193.0 + 126.0 * ALPHA_F) / 256.0,
        (105.0 + 302.0 * ALPHA_F) / 256.0,
        -15.0 * slack / 64.0,
        45.0 * slack / 512.0,
        -5.0 * slack / 256.0,
        slack / 512.0,
    ]


def split(table):
    table = np.asarray(table, np.float32)
    high = table.astype(ml_dtypes.bfloat16)
    low = (table - high.astype(np.float32)).astype(ml_dtypes.bfloat16)
    return high, low


def decay(alpha):
    return (-1.0 + np.sqrt(1.0 - 4.0 * alpha * alpha)) / (2.0 * alpha)


def azimuth_tables(cells, blocks):
    total = cells * blocks
    wave = 2.0 * np.pi * np.arange(total) / total
    slope_symbol = 1j * (COEF_A * np.sin(wave) + 0.5 * COEF_B * np.sin(2.0 * wave))
    slope_symbol = slope_symbol / (1.0 + 2.0 * ALPHA_D * np.cos(wave))
    weights = filter_weights()
    smooth_symbol = sum(w * np.cos(n * wave) for n, w in enumerate(weights))
    smooth_symbol = smooth_symbol / (1.0 + 2.0 * ALPHA_F * np.cos(wave))
    slope = np.real(np.fft.ifft(slope_symbol))
    smooth = np.real(np.fft.ifft(smooth_symbol))
    i = np.arange(cells)
    gap = (i[:, None] - i[None, :]) % total
    main = np.concatenate([slope[gap], smooth[gap]], axis=0)
    rate_d, rate_f = decay(ALPHA_D), decay(ALPHA_F)
    scale_d = slope[2] / rate_d**2
    scale_f = smooth[5] / rate_f**5
    send_right = np.zeros((EDGE, cells))
    send_right[0] = rate_d ** (cells - 1 - i)
    send_right[1] = rate_f ** (cells - 1 - i)
    use_left = np.zeros((2 * cells, EDGE))
    use_left[:cells, 0] = scale_d * rate_d ** (i + 1)
    use_left[cells:, 1] = scale_f * rate_f ** (i + 1)
    for m in range(EDGE - 2):
        send_right[2 + m, cells - 1 - m] = 1.0
        for row in range(EDGE - 2 - m):
            n = row + 1 + m
            if n < 2:
                use_left[row, 2 + m] = slope[n] - scale_d * rate_d**n
            if n < 5:
                use_left[cells + row, 2 + m] = smooth[n] - scale_f * rate_f**n
    send_left = send_right[:, ::-1]
    use_right = np.concatenate([-use_left[:cells][::-1], use_left[cells:][::-1]], axis=0)
    return main, send_right, send_left, use_left, use_right


def radial_matrix(total):
    system = np.eye(total) + ALPHA_D * (np.eye(total, k=1) + np.eye(total, k=-1))
    side = 0.5 * COEF_A * (np.eye(total, k=1) - np.eye(total, k=-1))
    side = side + 0.25 * COEF_B * (np.eye(total, k=2) - np.eye(total, k=-2))
    return np.linalg.solve(system, side)


def rank_two(corner):
    cells = corner.shape[0]
    send = np.zeros((2, cells))
    send[0] = corner[1] / corner[1, cells - 1]
    send[1, cells - 1] = 1.0
    use = np.zeros((cells, 2))
    use[1:, 0] = corner[1:, cells - 1]
    use[0, 0] = corner[0, cells - 2] / send[0, cells - 2]
    use[0, 1] = corner[0, cells - 1] - use[0, 0]
    return use, send


def radial_tables(cells, blocks):
    full = radial_matrix(cells * blocks).reshape(blocks, cells, blocks, cells)
    main = np.stack([full[b, :, b, :] for b in range(blocks)])
    use_left = np.zeros((blocks, cells, 2))
    use_right = np.zeros((blocks, cells, 2))
    send_right = np.zeros((blocks, 2, cells))
    send_left = np.zeros((blocks, 2, cells))
    for b in range(1, blocks):
        use_left[b], send_right[b - 1] = rank_two(full[b, :, b - 1, :])
    for b in range(blocks - 1):
        use, send = rank_two(full[b, :, b + 1, :][::-1, ::-1])
        use_right[b], send_left[b + 1] = use[::-1], send[:, ::-1]
    return main, send_right, send_left, use_left, use_right


def build_tables(cells_t, azi_count, cells_r, rad_count):
    main, send_right, send_left, use_left, use_right = azimuth_tables(cells_t, azi_count)
    sends = np.zeros((16, cells_t))
    sends[:EDGE], sends[8 : 8 + EDGE] = send_right, send_left
    high, low = split(sends)
    azi_send = np.concatenate([high, low, high], axis=1)
    uses = np.zeros((2 * cells_t, 16))
    uses[:, :EDGE], uses[:, 8 : 8 + EDGE] = use_left, use_right
    high, low = split(main)
    use_high, use_low = split(uses)
    azi_main = np.concatenate([high, low, high, use_high, use_low, use_high], axis=1)

    main, send_right, send_left, use_left, use_right = radial_tables(cells_r, rad_count)
    sends = np.concatenate([send_right, send_left], axis=1)
    high, low = split(sends)
    rad_send = np.zeros((rad_count, 16, 2 * cells_r), ml_dtypes.bfloat16)
    rad_send[:, 0:4, :cells_r] = high
    rad_send[:, 0:4, cells_r:] = high
    rad_send[:, 8:12, :cells_r] = low
    turned = np.swapaxes(main, 1, 2)
    high, low = split(turned)
    rad_main = np.zeros((rad_count, 2 * cells_r, 2 * cells_r), ml_dtypes.bfloat16)
    rad_main[:, :cells_r, :cells_r] = high
    rad_main[:, :cells_r, cells_r:] = low
    rad_main[:, cells_r:, :cells_r] = high
    uses = np.swapaxes(np.concatenate([use_left, use_right], axis=2), 1, 2)
    high, low = split(uses)
    rad_use = np.zeros((rad_count, 16, cells_r), ml_dtypes.bfloat16)
    rad_use[:, 0:4], rad_use[:, 4:8], rad_use[:, 8:12] = high, low, high
    return azi_send, azi_main, rad_send, rad_main, rad_use


def halves(x):
    high = x.astype(BF16)
    return high, (x - high.astype(F32)).astype(BF16)


def dot(a, b):
    return jnp.dot(a, b, preferred_element_type=F32)


def exchange_kernel(
    azi_count, rad_count, chunk,
    fields, azi_send, rad_send,
    from_left, from_right, from_in, from_out,
    block, to_right, to_left, to_out, to_in, load_sem, send_sem, recv_sem,
):
    planes, cells_t, cells_r = block.shape
    rad, azi = lax.axis_index("rad"), lax.axis_index("azi")
    right = (rad, lax.rem(azi + 1, azi_count))
    left = (rad, lax.rem(azi + azi_count - 1, azi_count))
    outer = (lax.rem(rad + 1, rad_count), azi)
    inner = (lax.rem(rad + rad_count - 1, rad_count), azi)
    barrier = pltpu.get_barrier_semaphore()
    for place in (right, left, outer, inner):
        pl.semaphore_signal(barrier, inc=1, device_id=place, device_id_type=MESH)
    count = planes // chunk
    loads = []
    for c in range(count):
        span = pl.ds(c * chunk, chunk)
        load = pltpu.make_async_copy(fields.at[span], block.at[span], load_sem.at[c])
        load.start()
        loads.append(load)
    radial_weights = rad_send[rad]
    for c in range(count):
        loads[c].wait()
        rows = chunk * cells_t
        high, low = halves(block[pl.ds(c * chunk, chunk)])
        pairs = jnp.concatenate([high.reshape(rows, cells_r), low.reshape(rows, cells_r)], axis=1)
        ends = lax.dot_general(
            radial_weights, pairs, (((1,), (1,)), ((), ())), preferred_element_type=F32
        )
        ends = ends[0:8] + ends[8:16]
        to_out[:, c * rows : (c + 1) * rows] = ends[0:2]
        to_in[:, c * rows : (c + 1) * rows] = ends[2:4]
        for p in range(chunk):
            stack = jnp.concatenate([high[p], high[p], low[p]], axis=0)
            edge = dot(azi_send[...], stack)
            group, slot = divmod(c * chunk + p, PACK)
            to_right[group, EDGE * slot : EDGE * (slot + 1), :] = edge[0:EDGE]
            to_left[group, EDGE * slot : EDGE * (slot + 1), :] = edge[8 : 8 + EDGE]
    pl.semaphore_wait(barrier, 4)
    copies = []
    for k, (source, target, place) in enumerate(
        (
            (to_right, from_left, right),
            (to_left, from_right, left),
            (to_out, from_in, outer),
            (to_in, from_out, inner),
        )
    ):
        copy = pltpu.make_async_remote_copy(
            src_ref=source,
            dst_ref=target,
            send_sem=send_sem.at[k],
            recv_sem=recv_sem.at[k],
            device_id=place,
            device_id_type=MESH,
        )
        copy.start()
        copies.append(copy)
    for copy in copies:
        copy.wait()


def solve_kernel(
    fields, from_left, from_right, from_in, from_out, azi_main, rad_main, rad_use,
    azimuth_metric, radial_metric,
    grad_azimuth, grad_radial, filtered,
    rims, ends,
):
    planes, cells_t, cells_r = fields.shape
    rad = lax.axis_index("rad")
    rows = planes * cells_t

    rims[...] = jnp.zeros_like(rims)
    ends[...] = jnp.zeros_like(ends)
    ends[0:2] = from_in[...]
    ends[2:4] = from_out[...]
    rim = ends[0:4]
    rim_high = rim.astype(BF16).astype(F32)
    ends[0:4] = rim_high
    ends[4:8] = rim_high
    ends[8:12] = rim - rim_high
    radial_rim = lax.dot_general(
        ends[...].astype(BF16), rad_use[rad], (((0,), (0,)), ((), ())), preferred_element_type=F32
    )
    high, low = halves(fields[...])
    pairs = jnp.concatenate([high.reshape(rows, cells_r), low.reshape(rows, cells_r)], axis=1)
    both = dot(pairs, rad_main[rad])
    slope = (both[:, :cells_r] + both[:, cells_r:] + radial_rim) * radial_metric[...]
    grad_radial[...] = slope.reshape(planes, cells_t, cells_r)
    for p in range(planes):
        group, slot = divmod(p, PACK)
        rims[p, 0:EDGE, :] = from_left[group, EDGE * slot : EDGE * (slot + 1), :]
        rims[p, 8 : 8 + EDGE, :] = from_right[group, EDGE * slot : EDGE * (slot + 1), :]
    for p in range(0, planes, 2):
        stacks = []
        for q in (p, p + 1):
            rim_h, rim_l = halves(rims[q])
            stacks.append(
                jnp.concatenate([high[q], high[q], low[q], rim_h, rim_h, rim_l], axis=0)
            )
        result = dot(azi_main[...], jnp.concatenate(stacks, axis=1))
        for k, q in enumerate((p, p + 1)):
            lanes = slice(k * cells_r, (k + 1) * cells_r)
            grad_azimuth[q] = result[:cells_t, lanes] * azimuth_metric[...]
            filtered[q] = result[cells_t:, lanes]


def local(tables, azi_count, rad_count, fields, radial_metric, azimuth_metric):
    azi_send, azi_main, rad_send, rad_main, rad_use = [jnp.asarray(t) for t in tables]
    shape = fields.shape
    cells_t, cells_r = shape[2], shape[3]
    planes = shape[0] * shape[1]
    x = fields.reshape(planes, cells_t, cells_r)
    chunk = 8
    steps = planes // chunk
    rims = jax.ShapeDtypeStruct((planes // PACK, PACK * EDGE, cells_r), F32)
    ends = jax.ShapeDtypeStruct((2, planes * cells_t), F32)
    hbm = pl.BlockSpec(memory_space=pl.ANY)
    vmem = pl.BlockSpec(memory_space=pltpu.VMEM)
    from_left, from_right, from_in, from_out = pl.pallas_call(
        functools.partial(exchange_kernel, azi_count, rad_count, chunk),
        out_shape=[rims, rims, ends, ends],
        in_specs=[hbm, vmem, vmem],
        out_specs=[hbm] * 4,
        scratch_shapes=[
            pltpu.VMEM(x.shape, F32),
            pltpu.VMEM(rims.shape, F32),
            pltpu.VMEM(rims.shape, F32),
            pltpu.VMEM(ends.shape, F32),
            pltpu.VMEM(ends.shape, F32),
            pltpu.SemaphoreType.DMA((steps,)),
            pltpu.SemaphoreType.DMA((4,)),
            pltpu.SemaphoreType.DMA((4,)),
        ],
        compiler_params=pltpu.CompilerParams(
            collective_id=0, has_side_effects=True, vmem_limit_bytes=32 * 2**20
        ),
    )(x, azi_send, rad_send)

    def whole(a):
        return pl.BlockSpec(a.shape, lambda i: (0,) * a.ndim)

    part = pl.BlockSpec((chunk, cells_t, cells_r), lambda i: (i, 0, 0))
    rim_part = pl.BlockSpec((chunk // PACK, PACK * EDGE, cells_r), lambda i: (i, 0, 0))
    end_part = pl.BlockSpec((2, chunk * cells_t), lambda i: (0, i))
    metrics = (azimuth_metric.reshape(1, cells_r), radial_metric.reshape(1, cells_r))
    outs = pl.pallas_call(
        solve_kernel,
        grid=(steps,),
        out_shape=[jax.ShapeDtypeStruct(x.shape, F32)] * 3,
        in_specs=[part, rim_part, rim_part, end_part, end_part]
        + [whole(a) for a in (azi_main, rad_main, rad_use) + metrics],
        out_specs=[part] * 3,
        scratch_shapes=[
            pltpu.VMEM((chunk, 16, cells_r), F32),
            pltpu.VMEM((16, chunk * cells_t), F32),
        ],
        compiler_params=pltpu.CompilerParams(vmem_limit_bytes=32 * 2**20),
    )(x, from_left, from_right, from_in, from_out, azi_main, rad_main, rad_use, *metrics)
    return tuple(a.reshape(shape) for a in outs)


def solution(mesh):
    rad_count, azi_count = mesh.shape["rad"], mesh.shape["azi"]
    spec = P(None, None, "azi", "rad")

    def run(fields, radial_metric, azimuth_metric):
        tables = build_tables(
            fields.shape[2] // azi_count, azi_count, fields.shape[3] // rad_count, rad_count
        )
        body = functools.partial(local, tables, azi_count, rad_count)
        return jax.shard_map(
            body,
            mesh=mesh,
            in_specs=(spec, P("rad"), P("rad")),
            out_specs=(spec, spec, spec),
            check_vma=False,
        )(fields, radial_metric, azimuth_metric)

    return run
```

```python
import functools

import jax
import jax.numpy as jnp
import ml_dtypes
import numpy as np
from jax import lax
from jax.experimental import pallas as pl
from jax.experimental.pallas import tpu as pltpu
from jax.sharding import PartitionSpec as P

ALPHA_D = 1.0 / 3.0
COEF_A = 14.0 / 9.0
COEF_B = 1.0 / 9.0
ALPHA_F = 0.49
MESH = pl.DeviceIdType.MESH
BF16 = jnp.bfloat16
F32 = jnp.float32

EDGE = 6
PACK = 4


def filter_weights():
    slack = 1.0 - 2.0 * ALPHA_F
    return [
        (193.0 + 126.0 * ALPHA_F) / 256.0,
        (105.0 + 302.0 * ALPHA_F) / 256.0,
        -15.0 * slack / 64.0,
        45.0 * slack / 512.0,
        -5.0 * slack / 256.0,
        slack / 512.0,
    ]


def split(table):
    table = np.asarray(table, np.float32)
    high = table.astype(ml_dtypes.bfloat16)
    low = (table - high.astype(np.float32)).astype(ml_dtypes.bfloat16)
    return high, low


def decay(alpha):
    return (-1.0 + np.sqrt(1.0 - 4.0 * alpha * alpha)) / (2.0 * alpha)


def azimuth_tables(cells, blocks):
    total = cells * blocks
    wave = 2.0 * np.pi * np.arange(total) / total
    slope_symbol = 1j * (COEF_A * np.sin(wave) + 0.5 * COEF_B * np.sin(2.0 * wave))
    slope_symbol = slope_symbol / (1.0 + 2.0 * ALPHA_D * np.cos(wave))
    weights = filter_weights()
    smooth_symbol = sum(w * np.cos(n * wave) for n, w in enumerate(weights))
    smooth_symbol = smooth_symbol / (1.0 + 2.0 * ALPHA_F * np.cos(wave))
    slope = np.real(np.fft.ifft(slope_symbol))
    smooth = np.real(np.fft.ifft(smooth_symbol))
    i = np.arange(cells)
    gap = (i[:, None] - i[None, :]) % total
    main = np.concatenate([slope[gap], smooth[gap]], axis=0)
    rate_d, rate_f = decay(ALPHA_D), decay(ALPHA_F)
    scale_d = slope[2] / rate_d**2
    scale_f = smooth[5] / rate_f**5
    send_right = np.zeros((EDGE, cells))
    send_right[0] = rate_d ** (cells - 1 - i)
    send_right[1] = rate_f ** (cells - 1 - i)
    use_left = np.zeros((2 * cells, EDGE))
    use_left[:cells, 0] = scale_d * rate_d ** (i + 1)
    use_left[cells:, 1] = scale_f * rate_f ** (i + 1)
    for m in range(EDGE - 2):
        send_right[2 + m, cells - 1 - m] = 1.0
        for row in range(EDGE - 2 - m):
            n = row + 1 + m
            if n < 2:
                use_left[row, 2 + m] = slope[n] - scale_d * rate_d**n
            if n < 5:
                use_left[cells + row, 2 + m] = smooth[n] - scale_f * rate_f**n
    send_left = send_right[:, ::-1]
    use_right = np.concatenate([-use_left[:cells][::-1], use_left[cells:][::-1]], axis=0)
    return main, send_right, send_left, use_left, use_right


def radial_matrix(total):
    system = np.eye(total) + ALPHA_D * (np.eye(total, k=1) + np.eye(total, k=-1))
    side = 0.5 * COEF_A * (np.eye(total, k=1) - np.eye(total, k=-1))
    side = side + 0.25 * COEF_B * (np.eye(total, k=2) - np.eye(total, k=-2))
    return np.linalg.solve(system, side)


def rank_two(corner):
    cells = corner.shape[0]
    send = np.zeros((2, cells))
    send[0] = corner[1] / corner[1, cells - 1]
    send[1, cells - 1] = 1.0
    use = np.zeros((cells, 2))
    use[1:, 0] = corner[1:, cells - 1]
    use[0, 0] = corner[0, cells - 2] / send[0, cells - 2]
    use[0, 1] = corner[0, cells - 1] - use[0, 0]
    return use, send


def radial_tables(cells, blocks):
    full = radial_matrix(cells * blocks).reshape(blocks, cells, blocks, cells)
    main = np.stack([full[b, :, b, :] for b in range(blocks)])
    use_left = np.zeros((blocks, cells, 2))
    use_right = np.zeros((blocks, cells, 2))
    send_right = np.zeros((blocks, 2, cells))
    send_left = np.zeros((blocks, 2, cells))
    for b in range(1, blocks):
        use_left[b], send_right[b - 1] = rank_two(full[b, :, b - 1, :])
    for b in range(blocks - 1):
        use, send = rank_two(full[b, :, b + 1, :][::-1, ::-1])
        use_right[b], send_left[b + 1] = use[::-1], send[:, ::-1]
    return main, send_right, send_left, use_left, use_right


def build_tables(cells_t, azi_count, cells_r, rad_count):
    main, send_right, send_left, use_left, use_right = azimuth_tables(cells_t, azi_count)
    sends = np.zeros((16, cells_t))
    sends[:EDGE], sends[8 : 8 + EDGE] = send_right, send_left
    high, low = split(sends)
    azi_send = np.concatenate([high, low, high], axis=1)
    uses = np.zeros((2 * cells_t, 16))
    uses[:, :EDGE], uses[:, 8 : 8 + EDGE] = use_left, use_right
    high, low = split(main)
    use_high, use_low = split(uses)
    azi_main = np.concatenate([high, low, high], axis=1)
    azi_use = np.concatenate([use_high, use_low, use_high], axis=1)

    main, send_right, send_left, use_left, use_right = radial_tables(cells_r, rad_count)
    sends = np.concatenate([send_right, send_left], axis=1)
    high, low = split(sends)
    rad_send = np.zeros((rad_count, 16, 2 * cells_r), ml_dtypes.bfloat16)
    rad_send[:, 0:4, :cells_r] = high
    rad_send[:, 0:4, cells_r:] = high
    rad_send[:, 8:12, :cells_r] = low
    turned = np.swapaxes(main, 1, 2)
    high, low = split(turned)
    rad_main = np.zeros((rad_count, 2 * cells_r, 2 * cells_r), ml_dtypes.bfloat16)
    rad_main[:, :cells_r, :cells_r] = high
    rad_main[:, :cells_r, cells_r:] = low
    rad_main[:, cells_r:, :cells_r] = high
    uses = np.swapaxes(np.concatenate([use_left, use_right], axis=2), 1, 2)
    high, low = split(uses)
    rad_use = np.zeros((rad_count, 16, cells_r), ml_dtypes.bfloat16)
    rad_use[:, 0:4], rad_use[:, 4:8], rad_use[:, 8:12] = high, low, high
    return azi_send, azi_main, azi_use, rad_send, rad_main, rad_use


def halves(x):
    high = x.astype(BF16)
    return high, (x - high.astype(F32)).astype(BF16)


def dot(a, b):
    return jnp.dot(a, b, preferred_element_type=F32)


def block_kernel(
    azi_count, rad_count, chunk,
    fields, azi_send, azi_main, rad_send, rad_main, rad_use, radial_metric,
    from_left, from_right, part_slope, part_smooth, grad_radial,
    block, azi_send_v, azi_main_v, rad_send_v, rad_main_v, rad_use_v, metric,
    to_right, to_left, to_out, to_in, from_in, from_out, ends,
    table_sem, load_sem, send_sem, recv_sem, rad_send_sem, rad_recv_sem,
):
    planes, cells_t, cells_r = block.shape
    count = planes // chunk
    rows = chunk * cells_t
    groups = chunk // PACK
    rad, azi = lax.axis_index("rad"), lax.axis_index("azi")
    right = (rad, lax.rem(azi + 1, azi_count))
    left = (rad, lax.rem(azi + azi_count - 1, azi_count))
    outer = (lax.rem(rad + 1, rad_count), azi)
    inner = (lax.rem(rad + rad_count - 1, rad_count), azi)
    barrier = pltpu.get_barrier_semaphore()
    for place in (right, left, outer, inner):
        pl.semaphore_signal(barrier, inc=1, device_id=place, device_id_type=MESH)

    def load(c):
        span = pl.ds(c * chunk, chunk)
        return pltpu.make_async_copy(fields.at[span], block.at[span], load_sem.at[c])

    tables = [
        pltpu.make_async_copy(source, target, table_sem.at[k])
        for k, (source, target) in enumerate(
            (
                (azi_send, azi_send_v),
                (rad_send.at[rad], rad_send_v),
                (azi_main, azi_main_v),
                (rad_main.at[rad], rad_main_v),
                (rad_use.at[rad], rad_use_v),
                (radial_metric, metric),
            )
        )
    ]
    tables[0].start()
    tables[1].start()
    for c in range(count):
        load(c).start()
    for table in tables[2:]:
        table.start()
    tables[0].wait()
    tables[1].wait()

    def sends(c):
        span = pl.ds(c * groups, groups)
        return [
            pltpu.make_async_remote_copy(
                src_ref=source.at[span],
                dst_ref=target.at[span],
                send_sem=send_sem.at[k, c],
                recv_sem=recv_sem.at[k, c],
                device_id=place,
                device_id_type=MESH,
            )
            for k, (source, target, place) in enumerate(
                ((to_right, from_left, right), (to_left, from_right, left))
            )
        ]

    def edges(c):
        load(c).wait()
        high, low = halves(block[pl.ds(c * chunk, chunk)])
        for p in range(0, chunk, 2):
            edge = dot(azi_send_v[...], stacked(high, low, p))
            for k in range(2):
                group, slot = divmod(p + k, PACK)
                lanes = slice(k * cells_r, (k + 1) * cells_r)
                span = slice(EDGE * slot, EDGE * (slot + 1))
                to_right[c * groups + group, span, :] = edge[0:EDGE, lanes]
                to_left[c * groups + group, span, :] = edge[8 : 8 + EDGE, lanes]

    def radial_edges(c):
        high, low = halves(block[pl.ds(c * chunk, chunk)])
        tips = lax.dot_general(
            rad_send_v[...], paired(high, low), (((1,), (1,)), ((), ())),
            preferred_element_type=F32,
        )
        tips = tips[0:8] + tips[8:16]
        span = pl.ds(pl.multiple_of(c * rows, rows), rows)
        to_out[:, span] = tips[0:2]
        to_in[:, span] = tips[2:4]

    edges(0)
    pl.semaphore_wait(barrier, 4)
    for copy in sends(0):
        copy.start()

    @pl.loop(1, count)
    def _(c):
        edges(c)
        for copy in sends(c):
            copy.start()

    @pl.loop(0, count)
    def _(c):
        radial_edges(c)

    radial_copies = [
        pltpu.make_async_remote_copy(
            src_ref=source,
            dst_ref=target,
            send_sem=rad_send_sem.at[k],
            recv_sem=rad_recv_sem.at[k],
            device_id=place,
            device_id_type=MESH,
        )
        for k, (source, target, place) in enumerate(
            ((to_out, from_in, outer), (to_in, from_out, inner))
        )
    ]
    for copy in radial_copies:
        copy.start()
    for table in tables[2:]:
        table.wait()
    ends[...] = jnp.zeros_like(ends)

    @pl.loop(0, count)
    def _(c):
        high, low = halves(block[pl.ds(c * chunk, chunk)])
        for p in range(0, chunk, 2):
            result = dot(azi_main_v[...], stacked(high, low, p))
            for k in range(2):
                lanes = slice(k * cells_r, (k + 1) * cells_r)
                part_slope[c * chunk + p + k] = result[:cells_t, lanes]
                part_smooth[c * chunk + p + k] = result[cells_t:, lanes]

    for copy in radial_copies:
        copy.wait()

    @pl.loop(0, count)
    def _(c):
        span = pl.ds(pl.multiple_of(c * rows, rows), rows)
        ends[0:2] = from_in[:, span]
        ends[2:4] = from_out[:, span]
        rim = ends[0:4]
        rim_high = rim.astype(BF16).astype(F32)
        ends[0:4] = rim_high
        ends[4:8] = rim_high
        ends[8:12] = rim - rim_high
        high, low = halves(block[pl.ds(c * chunk, chunk)])
        both = dot(paired(high, low), rad_main_v[...])
        outside = lax.dot_general(
            ends[...].astype(BF16), rad_use_v[...], (((0,), (0,)), ((), ())),
            preferred_element_type=F32,
        )
        slope = (both[:, :cells_r] + both[:, cells_r:] + outside) * metric[...]
        grad_radial[pl.ds(c * chunk, chunk)] = slope.reshape(chunk, cells_t, cells_r)

    @pl.loop(0, count)
    def _(c):
        for copy in sends(c):
            copy.wait()


def stacked(high, low, p):
    return jnp.concatenate(
        [jnp.concatenate([high[q], high[q], low[q]], axis=0) for q in (p, p + 1)], axis=1
    )


def paired(high, low):
    planes, cells_t, cells_r = high.shape
    rows = planes * cells_t
    return jnp.concatenate([high.reshape(rows, cells_r), low.reshape(rows, cells_r)], axis=1)


def join_kernel(
    chunk, part_slope, part_smooth, radial, from_left, from_right, azi_use, azimuth_metric,
    grad_azimuth, filtered, grad_radial,
    rims, sem,
):
    cells_t, cells_r = part_slope.shape[1:]
    step = pl.program_id(0)
    copy = pltpu.make_async_copy(radial, grad_radial, sem)

    @pl.when(step == 0)
    def _():
        copy.start()

    rims[...] = jnp.zeros_like(rims)
    for p in range(chunk):
        group, slot = divmod(p, PACK)
        group = step * (chunk // PACK) + group
        rims[p, 0:EDGE, :] = from_left[group, EDGE * slot : EDGE * (slot + 1), :]
        rims[p, 8 : 8 + EDGE, :] = from_right[group, EDGE * slot : EDGE * (slot + 1), :]
    high, low = halves(rims[...])
    for p in range(0, chunk, 2):
        result = dot(azi_use[...], stacked(high, low, p).astype(BF16))
        for k, q in enumerate((p, p + 1)):
            lanes = slice(k * cells_r, (k + 1) * cells_r)
            slope = part_slope[step * chunk + q] + result[:cells_t, lanes]
            grad_azimuth[q] = slope * azimuth_metric[...]
            filtered[q] = part_smooth[step * chunk + q] + result[cells_t:, lanes]

    @pl.when(step == pl.num_programs(0) - 1)
    def _():
        copy.wait()


def local(tables, azi_count, rad_count, fields, radial_metric, azimuth_metric):
    azi_send, azi_main, azi_use, rad_send, rad_main, rad_use = [jnp.asarray(t) for t in tables]
    shape = fields.shape
    cells_t, cells_r = shape[2], shape[3]
    planes = shape[0] * shape[1]
    x = fields.reshape(planes, cells_t, cells_r)
    chunk = 8
    count = planes // chunk
    rims = jax.ShapeDtypeStruct((planes // PACK, PACK * EDGE, cells_r), F32)
    full = jax.ShapeDtypeStruct(x.shape, F32)
    ends = pltpu.VMEM((2, planes * cells_t), F32)
    hbm = pl.BlockSpec(memory_space=pltpu.HBM)
    vmem = pl.BlockSpec(memory_space=pltpu.VMEM)
    dma = pltpu.SemaphoreType.DMA
    from_left, from_right, part_slope, part_smooth, radial = pl.pallas_call(
        functools.partial(block_kernel, azi_count, rad_count, chunk),
        out_shape=[rims, rims, full, full, full],
        in_specs=[hbm] * 7,
        out_specs=[vmem] * 5,
        scratch_shapes=[
            pltpu.VMEM(x.shape, F32),
            pltpu.VMEM(azi_send.shape, BF16),
            pltpu.VMEM(azi_main.shape, BF16),
            pltpu.VMEM(rad_send.shape[1:], BF16),
            pltpu.VMEM(rad_main.shape[1:], BF16),
            pltpu.VMEM(rad_use.shape[1:], BF16),
            pltpu.VMEM((1, cells_r), F32),
            pltpu.VMEM(rims.shape, F32),
            pltpu.VMEM(rims.shape, F32),
            ends,
            ends,
            ends,
            ends,
            pltpu.VMEM((16, chunk * cells_t), F32),
            dma((6,)),
            dma((count,)),
            dma((2, count)),
            dma((2, count)),
            dma((2,)),
            dma((2,)),
        ],
        compiler_params=pltpu.CompilerParams(
            collective_id=0, has_side_effects=True, vmem_limit_bytes=24 * 2**20
        ),
    )(
        *[
            pltpu.with_memory_space_constraint(a, pltpu.HBM)
            for a in (x, azi_send, azi_main, rad_send, rad_main, rad_use, radial_metric.reshape(1, cells_r))
        ]
    )

    part = pl.BlockSpec((chunk, cells_t, cells_r), lambda i: (i, 0, 0))
    outs = pl.pallas_call(
        functools.partial(join_kernel, chunk),
        grid=(count,),
        out_shape=[full] * 3,
        in_specs=[vmem] * 7,
        out_specs=[part, part, hbm],
        scratch_shapes=[pltpu.VMEM((chunk, 16, cells_r), F32), dma],
        compiler_params=pltpu.CompilerParams(vmem_limit_bytes=24 * 2**20),
    )(
        part_slope, part_smooth, radial, from_left, from_right, azi_use,
        azimuth_metric.reshape(1, cells_r),
    )
    grad_azimuth, filtered, grad_radial = [a.reshape(shape) for a in outs]
    return grad_azimuth, grad_radial, filtered


def solution(mesh):
    rad_count, azi_count = mesh.shape["rad"], mesh.shape["azi"]
    spec = P(None, None, "azi", "rad")

    def run(fields, radial_metric, azimuth_metric):
        tables = build_tables(
            fields.shape[2] // azi_count, azi_count, fields.shape[3] // rad_count, rad_count
        )
        body = functools.partial(local, tables, azi_count, rad_count)
        return jax.shard_map(
            body,
            mesh=mesh,
            in_specs=(spec, P("rad"), P("rad")),
            out_specs=(spec, spec, spec),
            check_vma=False,
        )(fields, radial_metric, azimuth_metric)

    return run
```

```python
import functools

import jax
import jax.numpy as jnp
import ml_dtypes
import numpy as np
from jax import lax
from jax.experimental import pallas as pl
from jax.experimental.pallas import tpu as pltpu
from jax.sharding import PartitionSpec as P

ALPHA_D = 1.0 / 3.0
COEF_A = 14.0 / 9.0
COEF_B = 1.0 / 9.0
ALPHA_F = 0.49
MESH = pl.DeviceIdType.MESH
BF16 = jnp.bfloat16
F32 = jnp.float32

EDGE = 6
PACK = 4


def filter_weights():
    slack = 1.0 - 2.0 * ALPHA_F
    return [
        (193.0 + 126.0 * ALPHA_F) / 256.0,
        (105.0 + 302.0 * ALPHA_F) / 256.0,
        -15.0 * slack / 64.0,
        45.0 * slack / 512.0,
        -5.0 * slack / 256.0,
        slack / 512.0,
    ]


def split(table):
    table = np.asarray(table, np.float32)
    high = table.astype(ml_dtypes.bfloat16)
    low = (table - high.astype(np.float32)).astype(ml_dtypes.bfloat16)
    return high, low


def decay(alpha):
    return (-1.0 + np.sqrt(1.0 - 4.0 * alpha * alpha)) / (2.0 * alpha)


def azimuth_tables(cells, blocks):
    total = cells * blocks
    wave = 2.0 * np.pi * np.arange(total) / total
    slope_symbol = 1j * (COEF_A * np.sin(wave) + 0.5 * COEF_B * np.sin(2.0 * wave))
    slope_symbol = slope_symbol / (1.0 + 2.0 * ALPHA_D * np.cos(wave))
    weights = filter_weights()
    smooth_symbol = sum(w * np.cos(n * wave) for n, w in enumerate(weights))
    smooth_symbol = smooth_symbol / (1.0 + 2.0 * ALPHA_F * np.cos(wave))
    slope = np.real(np.fft.ifft(slope_symbol))
    smooth = np.real(np.fft.ifft(smooth_symbol))
    i = np.arange(cells)
    gap = (i[:, None] - i[None, :]) % total
    main = np.concatenate([slope[gap], smooth[gap]], axis=0)
    rate_d, rate_f = decay(ALPHA_D), decay(ALPHA_F)
    scale_d = slope[2] / rate_d**2
    scale_f = smooth[5] / rate_f**5
    send_right = np.zeros((EDGE, cells))
    send_right[0] = rate_d ** (cells - 1 - i)
    send_right[1] = rate_f ** (cells - 1 - i)
    use_left = np.zeros((2 * cells, EDGE))
    use_left[:cells, 0] = scale_d * rate_d ** (i + 1)
    use_left[cells:, 1] = scale_f * rate_f ** (i + 1)
    for m in range(EDGE - 2):
        send_right[2 + m, cells - 1 - m] = 1.0
        for row in range(EDGE - 2 - m):
            n = row + 1 + m
            if n < 2:
                use_left[row, 2 + m] = slope[n] - scale_d * rate_d**n
            if n < 5:
                use_left[cells + row, 2 + m] = smooth[n] - scale_f * rate_f**n
    send_left = send_right[:, ::-1]
    use_right = np.concatenate([-use_left[:cells][::-1], use_left[cells:][::-1]], axis=0)
    return main, send_right, send_left, use_left, use_right


def radial_matrix(total):
    system = np.eye(total) + ALPHA_D * (np.eye(total, k=1) + np.eye(total, k=-1))
    side = 0.5 * COEF_A * (np.eye(total, k=1) - np.eye(total, k=-1))
    side = side + 0.25 * COEF_B * (np.eye(total, k=2) - np.eye(total, k=-2))
    return np.linalg.solve(system, side)


def rank_two(corner):
    cells = corner.shape[0]
    send = np.zeros((2, cells))
    send[0] = corner[1] / corner[1, cells - 1]
    send[1, cells - 1] = 1.0
    use = np.zeros((cells, 2))
    use[1:, 0] = corner[1:, cells - 1]
    use[0, 0] = corner[0, cells - 2] / send[0, cells - 2]
    use[0, 1] = corner[0, cells - 1] - use[0, 0]
    return use, send


def radial_tables(cells, blocks):
    full = radial_matrix(cells * blocks).reshape(blocks, cells, blocks, cells)
    main = np.stack([full[b, :, b, :] for b in range(blocks)])
    use_left = np.zeros((blocks, cells, 2))
    use_right = np.zeros((blocks, cells, 2))
    send_right = np.zeros((blocks, 2, cells))
    send_left = np.zeros((blocks, 2, cells))
    for b in range(1, blocks):
        use_left[b], send_right[b - 1] = rank_two(full[b, :, b - 1, :])
    for b in range(blocks - 1):
        use, send = rank_two(full[b, :, b + 1, :][::-1, ::-1])
        use_right[b], send_left[b + 1] = use[::-1], send[:, ::-1]
    return main, send_right, send_left, use_left, use_right


def build_tables(cells_t, azi_count, cells_r, rad_count):
    main, send_right, send_left, use_left, use_right = azimuth_tables(cells_t, azi_count)
    sends = np.zeros((16, cells_t))
    sends[:EDGE], sends[8 : 8 + EDGE] = send_right, send_left
    high, low = split(sends)
    azi_send = np.concatenate([high, low, high], axis=1)
    uses = np.zeros((2 * cells_t, 16))
    uses[:, :EDGE], uses[:, 8 : 8 + EDGE] = use_left, use_right
    high, low = split(main)
    use_high, use_low = split(uses)
    azi_main = np.concatenate([high, low, high], axis=1)
    azi_use = np.concatenate([use_high, use_low, use_high], axis=1)

    main, send_right, send_left, use_left, use_right = radial_tables(cells_r, rad_count)
    sends = np.concatenate([send_right, send_left], axis=1)
    high, low = split(sends)
    rad_send = np.zeros((rad_count, 16, 2 * cells_r), ml_dtypes.bfloat16)
    rad_send[:, 0:4, :cells_r] = high
    rad_send[:, 0:4, cells_r:] = high
    rad_send[:, 8:12, :cells_r] = low
    turned = np.swapaxes(main, 1, 2)
    high, low = split(turned)
    rad_main = np.zeros((rad_count, 2 * cells_r, 2 * cells_r), ml_dtypes.bfloat16)
    rad_main[:, :cells_r, :cells_r] = high
    rad_main[:, :cells_r, cells_r:] = low
    rad_main[:, cells_r:, :cells_r] = high
    uses = np.swapaxes(np.concatenate([use_left, use_right], axis=2), 1, 2)
    high, low = split(uses)
    rad_use = np.zeros((rad_count, 16, cells_r), ml_dtypes.bfloat16)
    rad_use[:, 0:4], rad_use[:, 4:8], rad_use[:, 8:12] = high, low, high
    return azi_send, azi_main, azi_use, rad_send, rad_main, rad_use


def halves(x):
    high = x.astype(BF16)
    return high, (x - high.astype(F32)).astype(BF16)


def dot(a, b):
    return jnp.dot(a, b, preferred_element_type=F32)


def block_kernel(
    azi_count, rad_count, chunk,
    fields, azi_send, azi_main, rad_send, rad_main, rad_use, radial_metric,
    from_left, from_right, part_slope, part_smooth, grad_radial,
    block, azi_send_v, azi_main_v, rad_send_v, rad_main_v, rad_use_v, metric,
    to_right, to_left, to_out, to_in, from_in, from_out, ends,
    table_sem, load_sem, send_sem, recv_sem, rad_send_sem, rad_recv_sem,
):
    planes, cells_t, cells_r = block.shape
    count = planes // chunk
    rows = chunk * cells_t
    groups = chunk // PACK
    rad, azi = lax.axis_index("rad"), lax.axis_index("azi")
    right = (rad, lax.rem(azi + 1, azi_count))
    left = (rad, lax.rem(azi + azi_count - 1, azi_count))
    outer = (lax.rem(rad + 1, rad_count), azi)
    inner = (lax.rem(rad + rad_count - 1, rad_count), azi)
    barrier = pltpu.get_barrier_semaphore()
    for place in (right, left, outer, inner):
        pl.semaphore_signal(barrier, inc=1, device_id=place, device_id_type=MESH)

    def load(c):
        span = pl.ds(c * chunk, chunk)
        return pltpu.make_async_copy(fields.at[span], block.at[span], load_sem.at[c])

    tables = [
        pltpu.make_async_copy(source, target, table_sem.at[k])
        for k, (source, target) in enumerate(
            (
                (azi_send, azi_send_v),
                (rad_send.at[rad], rad_send_v),
                (azi_main, azi_main_v),
                (rad_main.at[rad], rad_main_v),
                (rad_use.at[rad], rad_use_v),
                (radial_metric, metric),
            )
        )
    ]
    tables[0].start()
    tables[1].start()
    for c in range(count):
        load(c).start()
    for table in tables[2:]:
        table.start()
    tables[0].wait()
    tables[1].wait()

    def sends(c):
        span = pl.ds(c * groups, groups)
        return [
            pltpu.make_async_remote_copy(
                src_ref=source.at[span],
                dst_ref=target.at[span],
                send_sem=send_sem.at[k, c],
                recv_sem=recv_sem.at[k, c],
                device_id=place,
                device_id_type=MESH,
            )
            for k, (source, target, place) in enumerate(
                ((to_right, from_left, right), (to_left, from_right, left))
            )
        ]

    def edges(c):
        load(c).wait()
        high, low = halves(block[pl.ds(c * chunk, chunk)])
        for p in range(0, chunk, 2):
            edge = dot(azi_send_v[...], stacked(high, low, p))
            for k in range(2):
                group, slot = divmod(p + k, PACK)
                lanes = slice(k * cells_r, (k + 1) * cells_r)
                span = slice(EDGE * slot, EDGE * (slot + 1))
                to_right[c * groups + group, span, :] = edge[0:EDGE, lanes]
                to_left[c * groups + group, span, :] = edge[8 : 8 + EDGE, lanes]

    def radial_edges(c):
        high, low = halves(block[pl.ds(c * chunk, chunk)])
        tips = lax.dot_general(
            rad_send_v[...], paired(high, low), (((1,), (1,)), ((), ())),
            preferred_element_type=F32,
        )
        tips = tips[0:8] + tips[8:16]
        span = pl.ds(pl.multiple_of(c * rows, rows), rows)
        to_out[:, span] = tips[0:2]
        to_in[:, span] = tips[2:4]

    edges(0)
    pl.semaphore_wait(barrier, 4)
    sends(0)[0].start()

    @pl.loop(1, count)
    def _(c):
        edges(c)
        sends(c)[0].start()

    @pl.loop(0, count)
    def _(c):
        radial_edges(c)

    @pl.loop(0, count)
    def _(c):
        sends(c)[1].start()

    radial_copies = [
        pltpu.make_async_remote_copy(
            src_ref=source,
            dst_ref=target,
            send_sem=rad_send_sem.at[k],
            recv_sem=rad_recv_sem.at[k],
            device_id=place,
            device_id_type=MESH,
        )
        for k, (source, target, place) in enumerate(
            ((to_out, from_in, outer), (to_in, from_out, inner))
        )
    ]
    for copy in radial_copies:
        copy.start()
    for table in tables[2:]:
        table.wait()
    ends[...] = jnp.zeros_like(ends)

    @pl.loop(0, count)
    def _(c):
        high, low = halves(block[pl.ds(c * chunk, chunk)])
        for p in range(0, chunk, 2):
            result = dot(azi_main_v[...], stacked(high, low, p))
            for k in range(2):
                lanes = slice(k * cells_r, (k + 1) * cells_r)
                part_slope[c * chunk + p + k] = result[:cells_t, lanes]
                part_smooth[c * chunk + p + k] = result[cells_t:, lanes]

    for copy in radial_copies:
        copy.wait()

    @pl.loop(0, count)
    def _(c):
        span = pl.ds(pl.multiple_of(c * rows, rows), rows)
        ends[0:2] = from_in[:, span]
        ends[2:4] = from_out[:, span]
        rim = ends[0:4]
        rim_high = rim.astype(BF16).astype(F32)
        ends[0:4] = rim_high
        ends[4:8] = rim_high
        ends[8:12] = rim - rim_high
        high, low = halves(block[pl.ds(c * chunk, chunk)])
        both = dot(paired(high, low), rad_main_v[...])
        outside = lax.dot_general(
            ends[...].astype(BF16), rad_use_v[...], (((0,), (0,)), ((), ())),
            preferred_element_type=F32,
        )
        slope = (both[:, :cells_r] + both[:, cells_r:] + outside) * metric[...]
        grad_radial[pl.ds(c * chunk, chunk)] = slope.reshape(chunk, cells_t, cells_r)

    @pl.loop(0, count)
    def _(c):
        for copy in sends(c):
            copy.wait()


def stacked(high, low, p):
    return jnp.concatenate(
        [jnp.concatenate([high[q], high[q], low[q]], axis=0) for q in (p, p + 1)], axis=1
    )


def paired(high, low):
    planes, cells_t, cells_r = high.shape
    rows = planes * cells_t
    return jnp.concatenate([high.reshape(rows, cells_r), low.reshape(rows, cells_r)], axis=1)


def join_kernel(
    chunk, part_slope, part_smooth, radial, from_left, from_right, azi_use, azimuth_metric,
    grad_azimuth, filtered, grad_radial,
    slopes, smooths, rims, radial_sem, sems,
):
    planes, cells_t, cells_r = part_slope.shape
    count = planes // chunk
    groups = chunk // PACK
    radial_copy = pltpu.make_async_copy(radial, grad_radial, radial_sem)
    radial_copy.start()
    rims[...] = jnp.zeros_like(rims)

    def stores(c):
        span = pl.ds(c * chunk, chunk)
        return [
            pltpu.make_async_copy(source.at[span], target.at[span], sems.at[k, c])
            for k, (source, target) in enumerate(((slopes, grad_azimuth), (smooths, filtered)))
        ]

    @pl.loop(0, count)
    def _(c):
        for p in range(chunk):
            group, slot = divmod(p, PACK)
            span = slice(EDGE * slot, EDGE * (slot + 1))
            rims[p, 0:EDGE, :] = from_left[c * groups + group, span, :]
            rims[p, 8 : 8 + EDGE, :] = from_right[c * groups + group, span, :]
        high, low = halves(rims[...])
        for p in range(0, chunk, 2):
            result = dot(azi_use[...], stacked(high, low, p))
            for k in range(2):
                q = c * chunk + p + k
                lanes = slice(k * cells_r, (k + 1) * cells_r)
                slopes[q] = (part_slope[q] + result[:cells_t, lanes]) * azimuth_metric[...]
                smooths[q] = part_smooth[q] + result[cells_t:, lanes]
        for copy in stores(c):
            copy.start()

    @pl.loop(0, count)
    def _(c):
        for copy in stores(c):
            copy.wait()

    radial_copy.wait()


def local(tables, azi_count, rad_count, fields, radial_metric, azimuth_metric):
    azi_send, azi_main, azi_use, rad_send, rad_main, rad_use = [jnp.asarray(t) for t in tables]
    shape = fields.shape
    cells_t, cells_r = shape[2], shape[3]
    planes = shape[0] * shape[1]
    x = fields.reshape(planes, cells_t, cells_r)
    chunk = 8
    count = planes // chunk
    rims = jax.ShapeDtypeStruct((planes // PACK, PACK * EDGE, cells_r), F32)
    full = jax.ShapeDtypeStruct(x.shape, F32)
    ends = pltpu.VMEM((2, planes * cells_t), F32)
    hbm = pl.BlockSpec(memory_space=pltpu.HBM)
    vmem = pl.BlockSpec(memory_space=pltpu.VMEM)
    dma = pltpu.SemaphoreType.DMA
    from_left, from_right, part_slope, part_smooth, radial = pl.pallas_call(
        functools.partial(block_kernel, azi_count, rad_count, chunk),
        out_shape=[rims, rims, full, full, full],
        in_specs=[hbm] * 7,
        out_specs=[vmem] * 5,
        scratch_shapes=[
            pltpu.VMEM(x.shape, F32),
            pltpu.VMEM(azi_send.shape, BF16),
            pltpu.VMEM(azi_main.shape, BF16),
            pltpu.VMEM(rad_send.shape[1:], BF16),
            pltpu.VMEM(rad_main.shape[1:], BF16),
            pltpu.VMEM(rad_use.shape[1:], BF16),
            pltpu.VMEM((1, cells_r), F32),
            pltpu.VMEM(rims.shape, F32),
            pltpu.VMEM(rims.shape, F32),
            ends,
            ends,
            ends,
            ends,
            pltpu.VMEM((16, chunk * cells_t), F32),
            dma((6,)),
            dma((count,)),
            dma((2, count)),
            dma((2, count)),
            dma((2,)),
            dma((2,)),
        ],
        compiler_params=pltpu.CompilerParams(
            collective_id=0, has_side_effects=True, vmem_limit_bytes=24 * 2**20
        ),
    )(
        *[
            pltpu.with_memory_space_constraint(a, pltpu.HBM)
            for a in (x, azi_send, azi_main, rad_send, rad_main, rad_use, radial_metric.reshape(1, cells_r))
        ]
    )

    outs = pl.pallas_call(
        functools.partial(join_kernel, chunk),
        out_shape=[full] * 3,
        in_specs=[vmem] * 7,
        out_specs=[hbm] * 3,
        scratch_shapes=[
            pltpu.VMEM(x.shape, F32),
            pltpu.VMEM(x.shape, F32),
            pltpu.VMEM((chunk, 16, cells_r), F32),
            dma,
            dma((2, count)),
        ],
        compiler_params=pltpu.CompilerParams(vmem_limit_bytes=24 * 2**20),
    )(
        part_slope, part_smooth, radial, from_left, from_right, azi_use,
        azimuth_metric.reshape(1, cells_r),
    )
    grad_azimuth, filtered, grad_radial = [a.reshape(shape) for a in outs]
    return grad_azimuth, grad_radial, filtered


def solution(mesh):
    rad_count, azi_count = mesh.shape["rad"], mesh.shape["azi"]
    spec = P(None, None, "azi", "rad")

    def run(fields, radial_metric, azimuth_metric):
        tables = build_tables(
            fields.shape[2] // azi_count, azi_count, fields.shape[3] // rad_count, rad_count
        )
        body = functools.partial(local, tables, azi_count, rad_count)
        return jax.shard_map(
            body,
            mesh=mesh,
            in_specs=(spec, P("rad"), P("rad")),
            out_specs=(spec, spec, spec),
            check_vma=False,
        )(fields, radial_metric, azimuth_metric)

    return run
```

```python
import functools

import jax
import jax.numpy as jnp
import ml_dtypes
import numpy as np
from jax import lax
from jax.experimental import pallas as pl
from jax.experimental.pallas import tpu as pltpu
from jax.sharding import PartitionSpec as P

ALPHA_D = 1.0 / 3.0
COEF_A = 14.0 / 9.0
COEF_B = 1.0 / 9.0
ALPHA_F = 0.49
MESH = pl.DeviceIdType.MESH
BF16 = jnp.bfloat16
F32 = jnp.float32

EDGE = 6
PACK = 4


def filter_weights():
    slack = 1.0 - 2.0 * ALPHA_F
    return [
        (193.0 + 126.0 * ALPHA_F) / 256.0,
        (105.0 + 302.0 * ALPHA_F) / 256.0,
        -15.0 * slack / 64.0,
        45.0 * slack / 512.0,
        -5.0 * slack / 256.0,
        slack / 512.0,
    ]


def split(table):
    table = np.asarray(table, np.float32)
    high = table.astype(ml_dtypes.bfloat16)
    low = (table - high.astype(np.float32)).astype(ml_dtypes.bfloat16)
    return high, low


def decay(alpha):
    return (-1.0 + np.sqrt(1.0 - 4.0 * alpha * alpha)) / (2.0 * alpha)


def azimuth_tables(cells, blocks):
    total = cells * blocks
    wave = 2.0 * np.pi * np.arange(total) / total
    slope_symbol = 1j * (COEF_A * np.sin(wave) + 0.5 * COEF_B * np.sin(2.0 * wave))
    slope_symbol = slope_symbol / (1.0 + 2.0 * ALPHA_D * np.cos(wave))
    weights = filter_weights()
    smooth_symbol = sum(w * np.cos(n * wave) for n, w in enumerate(weights))
    smooth_symbol = smooth_symbol / (1.0 + 2.0 * ALPHA_F * np.cos(wave))
    slope = np.real(np.fft.ifft(slope_symbol))
    smooth = np.real(np.fft.ifft(smooth_symbol))
    i = np.arange(cells)
    gap = (i[:, None] - i[None, :]) % total
    main = np.concatenate([slope[gap], smooth[gap]], axis=0)
    rate_d, rate_f = decay(ALPHA_D), decay(ALPHA_F)
    scale_d = slope[2] / rate_d**2
    scale_f = smooth[5] / rate_f**5
    send_right = np.zeros((EDGE, cells))
    send_right[0] = rate_d ** (cells - 1 - i)
    send_right[1] = rate_f ** (cells - 1 - i)
    use_left = np.zeros((2 * cells, EDGE))
    use_left[:cells, 0] = scale_d * rate_d ** (i + 1)
    use_left[cells:, 1] = scale_f * rate_f ** (i + 1)
    for m in range(EDGE - 2):
        send_right[2 + m, cells - 1 - m] = 1.0
        for row in range(EDGE - 2 - m):
            n = row + 1 + m
            if n < 2:
                use_left[row, 2 + m] = slope[n] - scale_d * rate_d**n
            if n < 5:
                use_left[cells + row, 2 + m] = smooth[n] - scale_f * rate_f**n
    send_left = send_right[:, ::-1]
    use_right = np.concatenate([-use_left[:cells][::-1], use_left[cells:][::-1]], axis=0)
    return main, send_right, send_left, use_left, use_right


def radial_matrix(total):
    system = np.eye(total) + ALPHA_D * (np.eye(total, k=1) + np.eye(total, k=-1))
    side = 0.5 * COEF_A * (np.eye(total, k=1) - np.eye(total, k=-1))
    side = side + 0.25 * COEF_B * (np.eye(total, k=2) - np.eye(total, k=-2))
    return np.linalg.solve(system, side)


def rank_two(corner):
    cells = corner.shape[0]
    send = np.zeros((2, cells))
    send[0] = corner[1] / corner[1, cells - 1]
    send[1, cells - 1] = 1.0
    use = np.zeros((cells, 2))
    use[1:, 0] = corner[1:, cells - 1]
    use[0, 0] = corner[0, cells - 2] / send[0, cells - 2]
    use[0, 1] = corner[0, cells - 1] - use[0, 0]
    return use, send


def radial_tables(cells, blocks):
    full = radial_matrix(cells * blocks).reshape(blocks, cells, blocks, cells)
    main = np.stack([full[b, :, b, :] for b in range(blocks)])
    use_left = np.zeros((blocks, cells, 2))
    use_right = np.zeros((blocks, cells, 2))
    send_right = np.zeros((blocks, 2, cells))
    send_left = np.zeros((blocks, 2, cells))
    for b in range(1, blocks):
        use_left[b], send_right[b - 1] = rank_two(full[b, :, b - 1, :])
    for b in range(blocks - 1):
        use, send = rank_two(full[b, :, b + 1, :][::-1, ::-1])
        use_right[b], send_left[b + 1] = use[::-1], send[:, ::-1]
    return main, send_right, send_left, use_left, use_right


def build_tables(cells_t, azi_count, cells_r, rad_count):
    main, send_right, send_left, use_left, use_right = azimuth_tables(cells_t, azi_count)
    sends = np.zeros((16, cells_t))
    sends[:EDGE], sends[8 : 8 + EDGE] = send_right, send_left
    high, low = split(sends)
    azi_send = np.concatenate([high, low, high], axis=1)
    uses = np.zeros((2 * cells_t, 16))
    uses[:, :EDGE], uses[:, 8 : 8 + EDGE] = use_left, use_right
    high, low = split(main)
    use_high, use_low = split(uses)
    azi_main = np.concatenate([high, low, high], axis=1)
    azi_use = np.concatenate([use_high, use_low, use_high], axis=1)

    main, send_right, send_left, use_left, use_right = radial_tables(cells_r, rad_count)
    sends = np.concatenate([send_right, send_left], axis=1)
    high, low = split(sends)
    rad_send = np.zeros((rad_count, 16, 2 * cells_r), ml_dtypes.bfloat16)
    rad_send[:, 0:4, :cells_r] = high
    rad_send[:, 0:4, cells_r:] = high
    rad_send[:, 8:12, :cells_r] = low
    turned = np.swapaxes(main, 1, 2)
    high, low = split(turned)
    rad_main = np.zeros((rad_count, 2 * cells_r, 2 * cells_r), ml_dtypes.bfloat16)
    rad_main[:, :cells_r, :cells_r] = high
    rad_main[:, :cells_r, cells_r:] = low
    rad_main[:, cells_r:, :cells_r] = high
    uses = np.swapaxes(np.concatenate([use_left, use_right], axis=2), 1, 2)
    high, low = split(uses)
    rad_use = np.zeros((rad_count, 16, cells_r), ml_dtypes.bfloat16)
    rad_use[:, 0:4], rad_use[:, 4:8], rad_use[:, 8:12] = high, low, high
    return azi_send, azi_main, azi_use, rad_send, rad_main, rad_use


def halves(x):
    high = x.astype(BF16)
    return high, (x - high.astype(F32)).astype(BF16)


def dot(a, b):
    return jnp.dot(a, b, preferred_element_type=F32)


def block_kernel(
    azi_count, rad_count, chunk,
    fields, azi_send, azi_main, rad_send, rad_main, rad_use, radial_metric,
    from_left, from_right, part_slope, part_smooth, grad_radial,
    block, azi_send_v, azi_main_v, rad_send_v, rad_main_v, rad_use_v, metric,
    to_right, to_left, to_out, to_in, from_in, from_out, ends,
    table_sem, load_sem, send_sem, recv_sem, rad_send_sem, rad_recv_sem,
):
    planes, cells_t, cells_r = block.shape
    count = planes // chunk
    rows = chunk * cells_t
    groups = chunk // PACK
    rad, azi = lax.axis_index("rad"), lax.axis_index("azi")
    right = (rad, lax.rem(azi + 1, azi_count))
    left = (rad, lax.rem(azi + azi_count - 1, azi_count))
    outer = (lax.rem(rad + 1, rad_count), azi)
    inner = (lax.rem(rad + rad_count - 1, rad_count), azi)
    barrier = pltpu.get_barrier_semaphore()
    for place in (right, left, outer, inner):
        pl.semaphore_signal(barrier, inc=1, device_id=place, device_id_type=MESH)

    def load(c):
        span = pl.ds(c * chunk, chunk)
        return pltpu.make_async_copy(fields.at[span], block.at[span], load_sem.at[c])

    tables = [
        pltpu.make_async_copy(source, target, table_sem.at[k])
        for k, (source, target) in enumerate(
            (
                (azi_send, azi_send_v),
                (rad_send.at[rad], rad_send_v),
                (azi_main, azi_main_v),
                (rad_main.at[rad], rad_main_v),
                (rad_use.at[rad], rad_use_v),
                (radial_metric, metric),
            )
        )
    ]
    tables[0].start()
    tables[1].start()
    for c in range(count):
        load(c).start()
    for table in tables[2:]:
        table.start()
    tables[0].wait()
    tables[1].wait()

    cuts = [0, max(1, 2 * count // 5), count]

    def sends(part):
        span = pl.ds(cuts[part] * groups, (cuts[part + 1] - cuts[part]) * groups)
        return [
            pltpu.make_async_remote_copy(
                src_ref=source.at[span],
                dst_ref=target.at[span],
                send_sem=send_sem.at[k, part],
                recv_sem=recv_sem.at[k, part],
                device_id=place,
                device_id_type=MESH,
            )
            for k, (source, target, place) in enumerate(
                ((to_right, from_left, right), (to_left, from_right, left))
            )
        ]

    def edges(c):
        load(c).wait()
        high, low = halves(block[pl.ds(c * chunk, chunk)])
        for p in range(0, chunk, 2):
            edge = dot(azi_send_v[...], stacked(high, low, p))
            for k in range(2):
                group, slot = divmod(p + k, PACK)
                lanes = slice(k * cells_r, (k + 1) * cells_r)
                span = slice(EDGE * slot, EDGE * (slot + 1))
                to_right[c * groups + group, span, :] = edge[0:EDGE, lanes]
                to_left[c * groups + group, span, :] = edge[8 : 8 + EDGE, lanes]

    def radial_edges(c):
        high, low = halves(block[pl.ds(c * chunk, chunk)])
        tips = lax.dot_general(
            rad_send_v[...], paired(high, low), (((1,), (1,)), ((), ())),
            preferred_element_type=F32,
        )
        tips = tips[0:8] + tips[8:16]
        span = pl.ds(pl.multiple_of(c * rows, rows), rows)
        to_out[:, span] = tips[0:2]
        to_in[:, span] = tips[2:4]

    azimuth_copies = []
    for part in range(2):
        pl.loop(cuts[part], cuts[part + 1])(edges)
        if part == 0:
            pl.semaphore_wait(barrier, 4)
        for copy in sends(part):
            copy.start()
            azimuth_copies.append(copy)

    @pl.loop(0, count)
    def _(c):
        radial_edges(c)

    radial_copies = [
        pltpu.make_async_remote_copy(
            src_ref=source,
            dst_ref=target,
            send_sem=rad_send_sem.at[k],
            recv_sem=rad_recv_sem.at[k],
            device_id=place,
            device_id_type=MESH,
        )
        for k, (source, target, place) in enumerate(
            ((to_out, from_in, outer), (to_in, from_out, inner))
        )
    ]
    for copy in radial_copies:
        copy.start()
    for table in tables[2:]:
        table.wait()
    ends[...] = jnp.zeros_like(ends)

    @pl.loop(0, count)
    def _(c):
        high, low = halves(block[pl.ds(c * chunk, chunk)])
        for p in range(0, chunk, 2):
            result = dot(azi_main_v[...], stacked(high, low, p))
            for k in range(2):
                lanes = slice(k * cells_r, (k + 1) * cells_r)
                part_slope[c * chunk + p + k] = result[:cells_t, lanes]
                part_smooth[c * chunk + p + k] = result[cells_t:, lanes]

    for copy in radial_copies:
        copy.wait()

    @pl.loop(0, count)
    def _(c):
        span = pl.ds(pl.multiple_of(c * rows, rows), rows)
        ends[0:2] = from_in[:, span]
        ends[2:4] = from_out[:, span]
        rim = ends[0:4]
        rim_high = rim.astype(BF16).astype(F32)
        ends[0:4] = rim_high
        ends[4:8] = rim_high
        ends[8:12] = rim - rim_high
        high, low = halves(block[pl.ds(c * chunk, chunk)])
        both = dot(paired(high, low), rad_main_v[...])
        outside = lax.dot_general(
            ends[...].astype(BF16), rad_use_v[...], (((0,), (0,)), ((), ())),
            preferred_element_type=F32,
        )
        slope = (both[:, :cells_r] + both[:, cells_r:] + outside) * metric[...]
        grad_radial[pl.ds(c * chunk, chunk)] = slope.reshape(chunk, cells_t, cells_r)

    for copy in azimuth_copies:
        copy.wait()


def stacked(high, low, p):
    return jnp.concatenate(
        [jnp.concatenate([high[q], high[q], low[q]], axis=0) for q in (p, p + 1)], axis=1
    )


def paired(high, low):
    planes, cells_t, cells_r = high.shape
    rows = planes * cells_t
    return jnp.concatenate([high.reshape(rows, cells_r), low.reshape(rows, cells_r)], axis=1)


def join_kernel(
    chunk, part_slope, part_smooth, radial, from_left, from_right, azi_use, azimuth_metric,
    grad_azimuth, filtered, grad_radial,
    slopes, smooths, rims, radial_sem, sems,
):
    planes, cells_t, cells_r = part_slope.shape
    count = planes // chunk
    groups = chunk // PACK
    radial_copy = pltpu.make_async_copy(radial, grad_radial, radial_sem)
    radial_copy.start()
    rims[...] = jnp.zeros_like(rims)

    def stores(c):
        span = pl.ds(c * chunk, chunk)
        return [
            pltpu.make_async_copy(source.at[span], target.at[span], sems.at[k, c])
            for k, (source, target) in enumerate(((slopes, grad_azimuth), (smooths, filtered)))
        ]

    @pl.loop(0, count)
    def _(c):
        for p in range(chunk):
            group, slot = divmod(p, PACK)
            span = slice(EDGE * slot, EDGE * (slot + 1))
            rims[p, 0:EDGE, :] = from_left[c * groups + group, span, :]
            rims[p, 8 : 8 + EDGE, :] = from_right[c * groups + group, span, :]
        high, low = halves(rims[...])
        for p in range(0, chunk, 2):
            result = dot(azi_use[...], stacked(high, low, p))
            for k in range(2):
                q = c * chunk + p + k
                lanes = slice(k * cells_r, (k + 1) * cells_r)
                slopes[q] = (part_slope[q] + result[:cells_t, lanes]) * azimuth_metric[...]
                smooths[q] = part_smooth[q] + result[cells_t:, lanes]
        for copy in stores(c):
            copy.start()

    @pl.loop(0, count)
    def _(c):
        for copy in stores(c):
            copy.wait()

    radial_copy.wait()


def local(tables, azi_count, rad_count, fields, radial_metric, azimuth_metric):
    azi_send, azi_main, azi_use, rad_send, rad_main, rad_use = [jnp.asarray(t) for t in tables]
    shape = fields.shape
    cells_t, cells_r = shape[2], shape[3]
    planes = shape[0] * shape[1]
    x = fields.reshape(planes, cells_t, cells_r)
    chunk = 8
    count = planes // chunk
    rims = jax.ShapeDtypeStruct((planes // PACK, PACK * EDGE, cells_r), F32)
    full = jax.ShapeDtypeStruct(x.shape, F32)
    ends = pltpu.VMEM((2, planes * cells_t), F32)
    hbm = pl.BlockSpec(memory_space=pltpu.HBM)
    vmem = pl.BlockSpec(memory_space=pltpu.VMEM)
    dma = pltpu.SemaphoreType.DMA
    from_left, from_right, part_slope, part_smooth, radial = pl.pallas_call(
        functools.partial(block_kernel, azi_count, rad_count, chunk),
        out_shape=[rims, rims, full, full, full],
        in_specs=[hbm] * 7,
        out_specs=[vmem] * 5,
        scratch_shapes=[
            pltpu.VMEM(x.shape, F32),
            pltpu.VMEM(azi_send.shape, BF16),
            pltpu.VMEM(azi_main.shape, BF16),
            pltpu.VMEM(rad_send.shape[1:], BF16),
            pltpu.VMEM(rad_main.shape[1:], BF16),
            pltpu.VMEM(rad_use.shape[1:], BF16),
            pltpu.VMEM((1, cells_r), F32),
            pltpu.VMEM(rims.shape, F32),
            pltpu.VMEM(rims.shape, F32),
            ends,
            ends,
            ends,
            ends,
            pltpu.VMEM((16, chunk * cells_t), F32),
            dma((6,)),
            dma((count,)),
            dma((2, 2)),
            dma((2, 2)),
            dma((2,)),
            dma((2,)),
        ],
        compiler_params=pltpu.CompilerParams(
            collective_id=0, has_side_effects=True, vmem_limit_bytes=24 * 2**20
        ),
    )(
        *[
            pltpu.with_memory_space_constraint(a, pltpu.HBM)
            for a in (x, azi_send, azi_main, rad_send, rad_main, rad_use, radial_metric.reshape(1, cells_r))
        ]
    )

    outs = pl.pallas_call(
        functools.partial(join_kernel, chunk),
        out_shape=[full] * 3,
        in_specs=[vmem] * 7,
        out_specs=[hbm] * 3,
        scratch_shapes=[
            pltpu.VMEM(x.shape, F32),
            pltpu.VMEM(x.shape, F32),
            pltpu.VMEM((chunk, 16, cells_r), F32),
            dma,
            dma((2, count)),
        ],
        compiler_params=pltpu.CompilerParams(vmem_limit_bytes=24 * 2**20),
    )(
        part_slope, part_smooth, radial, from_left, from_right, azi_use,
        azimuth_metric.reshape(1, cells_r),
    )
    grad_azimuth, filtered, grad_radial = [a.reshape(shape) for a in outs]
    return grad_azimuth, grad_radial, filtered


def solution(mesh):
    rad_count, azi_count = mesh.shape["rad"], mesh.shape["azi"]
    spec = P(None, None, "azi", "rad")

    def run(fields, radial_metric, azimuth_metric):
        tables = build_tables(
            fields.shape[2] // azi_count, azi_count, fields.shape[3] // rad_count, rad_count
        )
        body = functools.partial(local, tables, azi_count, rad_count)
        return jax.shard_map(
            body,
            mesh=mesh,
            in_specs=(spec, P("rad"), P("rad")),
            out_specs=(spec, spec, spec),
            check_vma=False,
        )(fields, radial_metric, azimuth_metric)

    return run
```

```python
import functools

import jax
import jax.numpy as jnp
import ml_dtypes
import numpy as np
from jax import lax
from jax.experimental import pallas as pl
from jax.experimental.pallas import tpu as pltpu
from jax.sharding import PartitionSpec as P

ALPHA_D = 1.0 / 3.0
COEF_A = 14.0 / 9.0
COEF_B = 1.0 / 9.0
ALPHA_F = 0.49
MESH = pl.DeviceIdType.MESH
BF16 = jnp.bfloat16
F32 = jnp.float32

EDGE = 6
PACK = 4


def filter_weights():
    slack = 1.0 - 2.0 * ALPHA_F
    return [
        (193.0 + 126.0 * ALPHA_F) / 256.0,
        (105.0 + 302.0 * ALPHA_F) / 256.0,
        -15.0 * slack / 64.0,
        45.0 * slack / 512.0,
        -5.0 * slack / 256.0,
        slack / 512.0,
    ]


def split(table):
    table = np.asarray(table, np.float32)
    high = table.astype(ml_dtypes.bfloat16)
    low = (table - high.astype(np.float32)).astype(ml_dtypes.bfloat16)
    return high, low


def decay(alpha):
    return (-1.0 + np.sqrt(1.0 - 4.0 * alpha * alpha)) / (2.0 * alpha)


def azimuth_tables(cells, blocks):
    total = cells * blocks
    wave = 2.0 * np.pi * np.arange(total) / total
    slope_symbol = 1j * (COEF_A * np.sin(wave) + 0.5 * COEF_B * np.sin(2.0 * wave))
    slope_symbol = slope_symbol / (1.0 + 2.0 * ALPHA_D * np.cos(wave))
    weights = filter_weights()
    smooth_symbol = sum(w * np.cos(n * wave) for n, w in enumerate(weights))
    smooth_symbol = smooth_symbol / (1.0 + 2.0 * ALPHA_F * np.cos(wave))
    slope = np.real(np.fft.ifft(slope_symbol))
    smooth = np.real(np.fft.ifft(smooth_symbol))
    i = np.arange(cells)
    gap = (i[:, None] - i[None, :]) % total
    main = np.concatenate([slope[gap], smooth[gap]], axis=0)
    rate_d, rate_f = decay(ALPHA_D), decay(ALPHA_F)
    scale_d = slope[2] / rate_d**2
    scale_f = smooth[5] / rate_f**5
    send_right = np.zeros((EDGE, cells))
    send_right[0] = rate_d ** (cells - 1 - i)
    send_right[1] = rate_f ** (cells - 1 - i)
    use_left = np.zeros((2 * cells, EDGE))
    use_left[:cells, 0] = scale_d * rate_d ** (i + 1)
    use_left[cells:, 1] = scale_f * rate_f ** (i + 1)
    for m in range(EDGE - 2):
        send_right[2 + m, cells - 1 - m] = 1.0
        for row in range(EDGE - 2 - m):
            n = row + 1 + m
            if n < 2:
                use_left[row, 2 + m] = slope[n] - scale_d * rate_d**n
            if n < 5:
                use_left[cells + row, 2 + m] = smooth[n] - scale_f * rate_f**n
    send_left = send_right[:, ::-1]
    use_right = np.concatenate([-use_left[:cells][::-1], use_left[cells:][::-1]], axis=0)
    return main, send_right, send_left, use_left, use_right


def radial_matrix(total):
    system = np.eye(total) + ALPHA_D * (np.eye(total, k=1) + np.eye(total, k=-1))
    side = 0.5 * COEF_A * (np.eye(total, k=1) - np.eye(total, k=-1))
    side = side + 0.25 * COEF_B * (np.eye(total, k=2) - np.eye(total, k=-2))
    return np.linalg.solve(system, side)


def rank_two(corner):
    cells = corner.shape[0]
    send = np.zeros((2, cells))
    send[0] = corner[1] / corner[1, cells - 1]
    send[1, cells - 1] = 1.0
    use = np.zeros((cells, 2))
    use[1:, 0] = corner[1:, cells - 1]
    use[0, 0] = corner[0, cells - 2] / send[0, cells - 2]
    use[0, 1] = corner[0, cells - 1] - use[0, 0]
    return use, send


def radial_tables(cells, blocks):
    full = radial_matrix(cells * blocks).reshape(blocks, cells, blocks, cells)
    main = np.stack([full[b, :, b, :] for b in range(blocks)])
    use_left = np.zeros((blocks, cells, 2))
    use_right = np.zeros((blocks, cells, 2))
    send_right = np.zeros((blocks, 2, cells))
    send_left = np.zeros((blocks, 2, cells))
    for b in range(1, blocks):
        use_left[b], send_right[b - 1] = rank_two(full[b, :, b - 1, :])
    for b in range(blocks - 1):
        use, send = rank_two(full[b, :, b + 1, :][::-1, ::-1])
        use_right[b], send_left[b + 1] = use[::-1], send[:, ::-1]
    return main, send_right, send_left, use_left, use_right


def build_tables(cells_t, azi_count, cells_r, rad_count):
    main, send_right, send_left, use_left, use_right = azimuth_tables(cells_t, azi_count)
    sends = np.zeros((16, cells_t))
    sends[:EDGE], sends[8 : 8 + EDGE] = send_right, send_left
    high, low = split(sends)
    azi_send = np.concatenate([high, low, high], axis=1)
    uses = np.zeros((2 * cells_t, 16))
    uses[:, :EDGE], uses[:, 8 : 8 + EDGE] = use_left, use_right
    high, low = split(main)
    use_high, use_low = split(uses)
    azi_main = np.concatenate([high, low, high], axis=1)
    azi_use = np.concatenate([use_high, use_low, use_high], axis=1)

    main, send_right, send_left, use_left, use_right = radial_tables(cells_r, rad_count)
    sends = np.concatenate([send_right, send_left], axis=1)
    high, low = split(sends)
    rad_send = np.zeros((rad_count, 16, 2 * cells_r), ml_dtypes.bfloat16)
    rad_send[:, 0:4, :cells_r] = high
    rad_send[:, 0:4, cells_r:] = high
    rad_send[:, 8:12, :cells_r] = low
    turned = np.swapaxes(main, 1, 2)
    high, low = split(turned)
    rad_main = np.zeros((rad_count, 2 * cells_r, 2 * cells_r), ml_dtypes.bfloat16)
    rad_main[:, :cells_r, :cells_r] = high
    rad_main[:, :cells_r, cells_r:] = low
    rad_main[:, cells_r:, :cells_r] = high
    uses = np.swapaxes(np.concatenate([use_left, use_right], axis=2), 1, 2)
    high, low = split(uses)
    rad_use = np.zeros((rad_count, 16, cells_r), ml_dtypes.bfloat16)
    rad_use[:, 0:4], rad_use[:, 4:8], rad_use[:, 8:12] = high, low, high
    return azi_send, azi_main, azi_use, rad_send, rad_main, rad_use


def halves(x):
    high = x.astype(BF16)
    return high, (x - high.astype(F32)).astype(BF16)


def dot(a, b):
    return jnp.dot(a, b, preferred_element_type=F32)


def block_kernel(
    azi_count, rad_count, chunk,
    fields, azi_send, azi_main, rad_send, rad_main, rad_use, radial_metric,
    from_left, from_right, part_slope, part_smooth, grad_radial,
    block, azi_send_v, azi_main_v, rad_send_v, rad_main_v, rad_use_v, metric,
    to_right, to_left, to_out, to_in, from_in, from_out, ends,
    table_sem, load_sem, send_sem, recv_sem, rad_send_sem, rad_recv_sem,
):
    planes, cells_t, cells_r = block.shape
    count = planes // chunk
    rows = chunk * cells_t
    groups = chunk // PACK
    rad, azi = lax.axis_index("rad"), lax.axis_index("azi")
    right = (rad, lax.rem(azi + 1, azi_count))
    left = (rad, lax.rem(azi + azi_count - 1, azi_count))
    outer = (lax.rem(rad + 1, rad_count), azi)
    inner = (lax.rem(rad + rad_count - 1, rad_count), azi)
    barrier = pltpu.get_barrier_semaphore()
    for place in (right, left, outer, inner):
        pl.semaphore_signal(barrier, inc=1, device_id=place, device_id_type=MESH)

    def load(c):
        span = pl.ds(c * chunk, chunk)
        return pltpu.make_async_copy(fields.at[span], block.at[span], load_sem.at[c])

    tables = [
        pltpu.make_async_copy(source, target, table_sem.at[k])
        for k, (source, target) in enumerate(
            (
                (azi_send, azi_send_v),
                (rad_send.at[rad], rad_send_v),
                (azi_main, azi_main_v),
                (rad_main.at[rad], rad_main_v),
                (rad_use.at[rad], rad_use_v),
                (radial_metric, metric),
            )
        )
    ]
    tables[0].start()
    tables[1].start()
    for c in range(count):
        load(c).start()
    for table in tables[2:]:
        table.start()
    tables[0].wait()
    tables[1].wait()

    cuts = [0, max(1, 2 * count // 5), count]

    def sends(part):
        span = pl.ds(cuts[part] * groups, (cuts[part + 1] - cuts[part]) * groups)
        return [
            pltpu.make_async_remote_copy(
                src_ref=source.at[span],
                dst_ref=target.at[span],
                send_sem=send_sem.at[k, part],
                recv_sem=recv_sem.at[k, part],
                device_id=place,
                device_id_type=MESH,
            )
            for k, (source, target, place) in enumerate(
                ((to_right, from_left, right), (to_left, from_right, left))
            )
        ]

    def edges(c):
        load(c).wait()
        high, low = halves(block[pl.ds(c * chunk, chunk)])
        for p in range(0, chunk, 2):
            edge = dot(azi_send_v[...], stacked(high, low, p))
            for k in range(2):
                group, slot = divmod(p + k, PACK)
                lanes = slice(k * cells_r, (k + 1) * cells_r)
                span = slice(EDGE * slot, EDGE * (slot + 1))
                to_right[c * groups + group, span, :] = edge[0:EDGE, lanes]
                to_left[c * groups + group, span, :] = edge[8 : 8 + EDGE, lanes]

    def radial_edges(c):
        high, low = halves(block[pl.ds(c * chunk, chunk)])
        tips = lax.dot_general(
            rad_send_v[...], paired(high, low), (((1,), (1,)), ((), ())),
            preferred_element_type=F32,
        )
        tips = tips[0:8] + tips[8:16]
        span = pl.ds(pl.multiple_of(c * rows, rows), rows)
        to_out[:, span] = tips[0:2]
        to_in[:, span] = tips[2:4]

    azimuth_copies = []
    for part in range(2):
        pl.loop(cuts[part], cuts[part + 1])(edges)
        if part == 0:
            pl.semaphore_wait(barrier, 4)
        rightward, leftward = sends(part)
        azimuth_copies += [rightward, leftward]
        rightward.start()
        pl.when(azi != azi_count - 1)(leftward.start)

    @pl.loop(0, count)
    def _(c):
        radial_edges(c)

    radial_copies = [
        pltpu.make_async_remote_copy(
            src_ref=source,
            dst_ref=target,
            send_sem=rad_send_sem.at[k],
            recv_sem=rad_recv_sem.at[k],
            device_id=place,
            device_id_type=MESH,
        )
        for k, (source, target, place) in enumerate(
            ((to_out, from_in, outer), (to_in, from_out, inner))
        )
    ]
    for copy in radial_copies:
        copy.start()
    for table in tables[2:]:
        table.wait()
    ends[...] = jnp.zeros_like(ends)

    @pl.loop(0, count)
    def _(c):
        high, low = halves(block[pl.ds(c * chunk, chunk)])
        for p in range(0, chunk, 2):
            result = dot(azi_main_v[...], stacked(high, low, p))
            for k in range(2):
                lanes = slice(k * cells_r, (k + 1) * cells_r)
                part_slope[c * chunk + p + k] = result[:cells_t, lanes]
                part_smooth[c * chunk + p + k] = result[cells_t:, lanes]

    for leftward in azimuth_copies[1::2]:
        pl.when(azi == azi_count - 1)(leftward.start)
    for copy in radial_copies:
        copy.wait()

    @pl.loop(0, count)
    def _(c):
        span = pl.ds(pl.multiple_of(c * rows, rows), rows)
        ends[0:2] = from_in[:, span]
        ends[2:4] = from_out[:, span]
        rim = ends[0:4]
        rim_high = rim.astype(BF16).astype(F32)
        ends[0:4] = rim_high
        ends[4:8] = rim_high
        ends[8:12] = rim - rim_high
        high, low = halves(block[pl.ds(c * chunk, chunk)])
        both = dot(paired(high, low), rad_main_v[...])
        outside = lax.dot_general(
            ends[...].astype(BF16), rad_use_v[...], (((0,), (0,)), ((), ())),
            preferred_element_type=F32,
        )
        slope = (both[:, :cells_r] + both[:, cells_r:] + outside) * metric[...]
        grad_radial[pl.ds(c * chunk, chunk)] = slope.reshape(chunk, cells_t, cells_r)

    for copy in azimuth_copies:
        copy.wait()


def stacked(high, low, p):
    return jnp.concatenate(
        [jnp.concatenate([high[q], high[q], low[q]], axis=0) for q in (p, p + 1)], axis=1
    )


def paired(high, low):
    planes, cells_t, cells_r = high.shape
    rows = planes * cells_t
    return jnp.concatenate([high.reshape(rows, cells_r), low.reshape(rows, cells_r)], axis=1)


def join_kernel(
    chunk, part_slope, part_smooth, radial, from_left, from_right, azi_use, azimuth_metric,
    grad_azimuth, filtered, grad_radial,
    slopes, smooths, rims, radial_sem, sems,
):
    planes, cells_t, cells_r = part_slope.shape
    count = planes // chunk
    groups = chunk // PACK
    radial_copy = pltpu.make_async_copy(radial, grad_radial, radial_sem)
    radial_copy.start()
    rims[...] = jnp.zeros_like(rims)

    def stores(c):
        span = pl.ds(c * chunk, chunk)
        return [
            pltpu.make_async_copy(source.at[span], target.at[span], sems.at[k, c])
            for k, (source, target) in enumerate(((slopes, grad_azimuth), (smooths, filtered)))
        ]

    @pl.loop(0, count)
    def _(c):
        for p in range(chunk):
            group, slot = divmod(p, PACK)
            span = slice(EDGE * slot, EDGE * (slot + 1))
            rims[p, 0:EDGE, :] = from_left[c * groups + group, span, :]
            rims[p, 8 : 8 + EDGE, :] = from_right[c * groups + group, span, :]
        high, low = halves(rims[...])
        for p in range(0, chunk, 2):
            result = dot(azi_use[...], stacked(high, low, p))
            for k in range(2):
                q = c * chunk + p + k
                lanes = slice(k * cells_r, (k + 1) * cells_r)
                slopes[q] = (part_slope[q] + result[:cells_t, lanes]) * azimuth_metric[...]
                smooths[q] = part_smooth[q] + result[cells_t:, lanes]
        for copy in stores(c):
            copy.start()

    @pl.loop(0, count)
    def _(c):
        for copy in stores(c):
            copy.wait()

    radial_copy.wait()


def local(tables, azi_count, rad_count, fields, radial_metric, azimuth_metric):
    azi_send, azi_main, azi_use, rad_send, rad_main, rad_use = [jnp.asarray(t) for t in tables]
    shape = fields.shape
    cells_t, cells_r = shape[2], shape[3]
    planes = shape[0] * shape[1]
    x = fields.reshape(planes, cells_t, cells_r)
    chunk = 8
    count = planes // chunk
    rims = jax.ShapeDtypeStruct((planes // PACK, PACK * EDGE, cells_r), F32)
    full = jax.ShapeDtypeStruct(x.shape, F32)
    ends = pltpu.VMEM((2, planes * cells_t), F32)
    hbm = pl.BlockSpec(memory_space=pltpu.HBM)
    vmem = pl.BlockSpec(memory_space=pltpu.VMEM)
    dma = pltpu.SemaphoreType.DMA
    from_left, from_right, part_slope, part_smooth, radial = pl.pallas_call(
        functools.partial(block_kernel, azi_count, rad_count, chunk),
        out_shape=[rims, rims, full, full, full],
        in_specs=[hbm] * 7,
        out_specs=[vmem] * 5,
        scratch_shapes=[
            pltpu.VMEM(x.shape, F32),
            pltpu.VMEM(azi_send.shape, BF16),
            pltpu.VMEM(azi_main.shape, BF16),
            pltpu.VMEM(rad_send.shape[1:], BF16),
            pltpu.VMEM(rad_main.shape[1:], BF16),
            pltpu.VMEM(rad_use.shape[1:], BF16),
            pltpu.VMEM((1, cells_r), F32),
            pltpu.VMEM(rims.shape, F32),
            pltpu.VMEM(rims.shape, F32),
            ends,
            ends,
            ends,
            ends,
            pltpu.VMEM((16, chunk * cells_t), F32),
            dma((6,)),
            dma((count,)),
            dma((2, 2)),
            dma((2, 2)),
            dma((2,)),
            dma((2,)),
        ],
        compiler_params=pltpu.CompilerParams(
            collective_id=0, has_side_effects=True, vmem_limit_bytes=24 * 2**20
        ),
    )(
        *[
            pltpu.with_memory_space_constraint(a, pltpu.HBM)
            for a in (x, azi_send, azi_main, rad_send, rad_main, rad_use, radial_metric.reshape(1, cells_r))
        ]
    )

    outs = pl.pallas_call(
        functools.partial(join_kernel, chunk),
        out_shape=[full] * 3,
        in_specs=[vmem] * 7,
        out_specs=[hbm] * 3,
        scratch_shapes=[
            pltpu.VMEM(x.shape, F32),
            pltpu.VMEM(x.shape, F32),
            pltpu.VMEM((chunk, 16, cells_r), F32),
            dma,
            dma((2, count)),
        ],
        compiler_params=pltpu.CompilerParams(vmem_limit_bytes=24 * 2**20),
    )(
        part_slope, part_smooth, radial, from_left, from_right, azi_use,
        azimuth_metric.reshape(1, cells_r),
    )
    grad_azimuth, filtered, grad_radial = [a.reshape(shape) for a in outs]
    return grad_azimuth, grad_radial, filtered


def solution(mesh):
    rad_count, azi_count = mesh.shape["rad"], mesh.shape["azi"]
    spec = P(None, None, "azi", "rad")

    def run(fields, radial_metric, azimuth_metric):
        tables = build_tables(
            fields.shape[2] // azi_count, azi_count, fields.shape[3] // rad_count, rad_count
        )
        body = functools.partial(local, tables, azi_count, rad_count)
        return jax.shard_map(
            body,
            mesh=mesh,
            in_specs=(spec, P("rad"), P("rad")),
            out_specs=(spec, spec, spec),
            check_vma=False,
        )(fields, radial_metric, azimuth_metric)

    return run
```

```python
import functools

import jax
import jax.numpy as jnp
import ml_dtypes
import numpy as np
from jax import lax
from jax.experimental import pallas as pl
from jax.experimental.pallas import tpu as pltpu
from jax.sharding import PartitionSpec as P

ALPHA_D = 1.0 / 3.0
COEF_A = 14.0 / 9.0
COEF_B = 1.0 / 9.0
ALPHA_F = 0.49
MESH = pl.DeviceIdType.MESH
BF16 = jnp.bfloat16
F32 = jnp.float32

EDGE = 6
PACK = 4


def filter_weights():
    slack = 1.0 - 2.0 * ALPHA_F
    return [
        (193.0 + 126.0 * ALPHA_F) / 256.0,
        (105.0 + 302.0 * ALPHA_F) / 256.0,
        -15.0 * slack / 64.0,
        45.0 * slack / 512.0,
        -5.0 * slack / 256.0,
        slack / 512.0,
    ]


def split(table):
    table = np.asarray(table, np.float32)
    high = table.astype(ml_dtypes.bfloat16)
    low = (table - high.astype(np.float32)).astype(ml_dtypes.bfloat16)
    return high, low


def decay(alpha):
    return (-1.0 + np.sqrt(1.0 - 4.0 * alpha * alpha)) / (2.0 * alpha)


def azimuth_tables(cells, blocks):
    total = cells * blocks
    wave = 2.0 * np.pi * np.arange(total) / total
    slope_symbol = 1j * (COEF_A * np.sin(wave) + 0.5 * COEF_B * np.sin(2.0 * wave))
    slope_symbol = slope_symbol / (1.0 + 2.0 * ALPHA_D * np.cos(wave))
    weights = filter_weights()
    smooth_symbol = sum(w * np.cos(n * wave) for n, w in enumerate(weights))
    smooth_symbol = smooth_symbol / (1.0 + 2.0 * ALPHA_F * np.cos(wave))
    slope = np.real(np.fft.ifft(slope_symbol))
    smooth = np.real(np.fft.ifft(smooth_symbol))
    i = np.arange(cells)
    gap = (i[:, None] - i[None, :]) % total
    main = np.concatenate([slope[gap], smooth[gap]], axis=0)
    rate_d, rate_f = decay(ALPHA_D), decay(ALPHA_F)
    scale_d = slope[2] / rate_d**2
    scale_f = smooth[5] / rate_f**5
    send_right = np.zeros((EDGE, cells))
    send_right[0] = rate_d ** (cells - 1 - i)
    send_right[1] = rate_f ** (cells - 1 - i)
    use_left = np.zeros((2 * cells, EDGE))
    use_left[:cells, 0] = scale_d * rate_d ** (i + 1)
    use_left[cells:, 1] = scale_f * rate_f ** (i + 1)
    for m in range(EDGE - 2):
        send_right[2 + m, cells - 1 - m] = 1.0
        for row in range(EDGE - 2 - m):
            n = row + 1 + m
            if n < 2:
                use_left[row, 2 + m] = slope[n] - scale_d * rate_d**n
            if n < 5:
                use_left[cells + row, 2 + m] = smooth[n] - scale_f * rate_f**n
    send_left = send_right[:, ::-1]
    use_right = np.concatenate([-use_left[:cells][::-1], use_left[cells:][::-1]], axis=0)
    return main, send_right, send_left, use_left, use_right


def radial_matrix(total):
    system = np.eye(total) + ALPHA_D * (np.eye(total, k=1) + np.eye(total, k=-1))
    side = 0.5 * COEF_A * (np.eye(total, k=1) - np.eye(total, k=-1))
    side = side + 0.25 * COEF_B * (np.eye(total, k=2) - np.eye(total, k=-2))
    return np.linalg.solve(system, side)


def rank_two(corner):
    cells = corner.shape[0]
    send = np.zeros((2, cells))
    send[0] = corner[1] / corner[1, cells - 1]
    send[1, cells - 1] = 1.0
    use = np.zeros((cells, 2))
    use[1:, 0] = corner[1:, cells - 1]
    use[0, 0] = corner[0, cells - 2] / send[0, cells - 2]
    use[0, 1] = corner[0, cells - 1] - use[0, 0]
    return use, send


def radial_tables(cells, blocks):
    full = radial_matrix(cells * blocks).reshape(blocks, cells, blocks, cells)
    main = np.stack([full[b, :, b, :] for b in range(blocks)])
    use_left = np.zeros((blocks, cells, 2))
    use_right = np.zeros((blocks, cells, 2))
    send_right = np.zeros((blocks, 2, cells))
    send_left = np.zeros((blocks, 2, cells))
    for b in range(1, blocks):
        use_left[b], send_right[b - 1] = rank_two(full[b, :, b - 1, :])
    for b in range(blocks - 1):
        use, send = rank_two(full[b, :, b + 1, :][::-1, ::-1])
        use_right[b], send_left[b + 1] = use[::-1], send[:, ::-1]
    return main, send_right, send_left, use_left, use_right


def build_tables(cells_t, azi_count, cells_r, rad_count):
    main, send_right, send_left, use_left, use_right = azimuth_tables(cells_t, azi_count)
    sends = np.zeros((16, cells_t))
    sends[:EDGE], sends[8 : 8 + EDGE] = send_right, send_left
    high, low = split(sends)
    azi_send = np.concatenate([high, low, high], axis=1)
    uses = np.zeros((2 * cells_t, 16))
    uses[:, :EDGE], uses[:, 8 : 8 + EDGE] = use_left, use_right
    high, low = split(main)
    use_high, use_low = split(uses)
    azi_main = np.concatenate([high, low, high], axis=1)
    azi_use = np.concatenate([use_high, use_low, use_high], axis=1)

    main, send_right, send_left, use_left, use_right = radial_tables(cells_r, rad_count)
    sends = np.concatenate([send_right, send_left], axis=1)
    high, low = split(sends)
    rad_send = np.zeros((rad_count, 16, 2 * cells_r), ml_dtypes.bfloat16)
    rad_send[:, 0:4, :cells_r] = high
    rad_send[:, 0:4, cells_r:] = high
    rad_send[:, 8:12, :cells_r] = low
    turned = np.swapaxes(main, 1, 2)
    high, low = split(turned)
    rad_main = np.zeros((rad_count, 2 * cells_r, 2 * cells_r), ml_dtypes.bfloat16)
    rad_main[:, :cells_r, :cells_r] = high
    rad_main[:, :cells_r, cells_r:] = low
    rad_main[:, cells_r:, :cells_r] = high
    uses = np.swapaxes(np.concatenate([use_left, use_right], axis=2), 1, 2)
    high, low = split(uses)
    rad_use = np.zeros((rad_count, 16, cells_r), ml_dtypes.bfloat16)
    rad_use[:, 0:4], rad_use[:, 4:8], rad_use[:, 8:12] = high, low, high
    return azi_send, azi_main, azi_use, rad_send, rad_main, rad_use


def halves(x):
    high = x.astype(BF16)
    return high, (x - high.astype(F32)).astype(BF16)


def dot(a, b):
    return jnp.dot(a, b, preferred_element_type=F32)


def block_kernel(
    azi_count, rad_count, chunk,
    fields, azi_send, azi_main, rad_send, rad_main, rad_use, radial_metric,
    from_left, from_right, part_slope, part_smooth, grad_radial,
    block, azi_send_v, azi_main_v, rad_send_v, rad_main_v, rad_use_v, metric,
    to_right, to_left, to_out, to_in, from_in, from_out, ends,
    table_sem, load_sem, send_sem, recv_sem, rad_send_sem, rad_recv_sem,
):
    planes, cells_t, cells_r = block.shape
    count = planes // chunk
    rows = chunk * cells_t
    groups = chunk // PACK
    rad, azi = lax.axis_index("rad"), lax.axis_index("azi")
    right = (rad, lax.rem(azi + 1, azi_count))
    left = (rad, lax.rem(azi + azi_count - 1, azi_count))
    outer = (lax.rem(rad + 1, rad_count), azi)
    inner = (lax.rem(rad + rad_count - 1, rad_count), azi)
    barrier = pltpu.get_barrier_semaphore()
    for place in (right, left, outer, inner):
        pl.semaphore_signal(barrier, inc=1, device_id=place, device_id_type=MESH)

    def load(c):
        span = pl.ds(c * chunk, chunk)
        return pltpu.make_async_copy(fields.at[span], block.at[span], load_sem.at[c])

    tables = [
        pltpu.make_async_copy(source, target, table_sem.at[k])
        for k, (source, target) in enumerate(
            (
                (azi_send, azi_send_v),
                (rad_send.at[rad], rad_send_v),
                (azi_main, azi_main_v),
                (rad_main.at[rad], rad_main_v),
                (rad_use.at[rad], rad_use_v),
                (radial_metric, metric),
            )
        )
    ]
    tables[0].start()
    tables[1].start()
    for c in range(count):
        load(c).start()
    for table in tables[2:]:
        table.start()
    tables[0].wait()
    tables[1].wait()

    cuts = [0, count]

    def sends(part):
        span = pl.ds(cuts[part] * groups, (cuts[part + 1] - cuts[part]) * groups)
        return [
            pltpu.make_async_remote_copy(
                src_ref=source.at[span],
                dst_ref=target.at[span],
                send_sem=send_sem.at[k, part],
                recv_sem=recv_sem.at[k, part],
                device_id=place,
                device_id_type=MESH,
            )
            for k, (source, target, place) in enumerate(
                ((to_right, from_left, right), (to_left, from_right, left))
            )
        ]

    def edges(c):
        load(c).wait()
        high, low = halves(block[pl.ds(c * chunk, chunk)])
        for p in range(0, chunk, 2):
            edge = dot(azi_send_v[...], stacked(high, low, p))
            for k in range(2):
                group, slot = divmod(p + k, PACK)
                lanes = slice(k * cells_r, (k + 1) * cells_r)
                span = slice(EDGE * slot, EDGE * (slot + 1))
                to_right[c * groups + group, span, :] = edge[0:EDGE, lanes]
                to_left[c * groups + group, span, :] = edge[8 : 8 + EDGE, lanes]

    def radial_edges(c):
        high, low = halves(block[pl.ds(c * chunk, chunk)])
        tips = lax.dot_general(
            rad_send_v[...], paired(high, low), (((1,), (1,)), ((), ())),
            preferred_element_type=F32,
        )
        tips = tips[0:8] + tips[8:16]
        span = pl.ds(pl.multiple_of(c * rows, rows), rows)
        to_out[:, span] = tips[0:2]
        to_in[:, span] = tips[2:4]

    azimuth_copies = []
    for part in range(len(cuts) - 1):
        pl.loop(cuts[part], cuts[part + 1])(edges)
        if part == 0:
            pl.semaphore_wait(barrier, 4)
        for copy in sends(part):
            copy.start()
            azimuth_copies.append(copy)

    @pl.loop(0, count)
    def _(c):
        radial_edges(c)

    radial_copies = [
        pltpu.make_async_remote_copy(
            src_ref=source,
            dst_ref=target,
            send_sem=rad_send_sem.at[k],
            recv_sem=rad_recv_sem.at[k],
            device_id=place,
            device_id_type=MESH,
        )
        for k, (source, target, place) in enumerate(
            ((to_out, from_in, outer), (to_in, from_out, inner))
        )
    ]
    for copy in radial_copies:
        copy.start()
    for table in tables[2:]:
        table.wait()
    ends[...] = jnp.zeros_like(ends)

    @pl.loop(0, count)
    def _(c):
        high, low = halves(block[pl.ds(c * chunk, chunk)])
        for p in range(0, chunk, 2):
            result = dot(azi_main_v[...], stacked(high, low, p))
            for k in range(2):
                lanes = slice(k * cells_r, (k + 1) * cells_r)
                part_slope[c * chunk + p + k] = result[:cells_t, lanes]
                part_smooth[c * chunk + p + k] = result[cells_t:, lanes]

    for copy in radial_copies:
        copy.wait()

    @pl.loop(0, count)
    def _(c):
        span = pl.ds(pl.multiple_of(c * rows, rows), rows)
        ends[0:2] = from_in[:, span]
        ends[2:4] = from_out[:, span]
        rim = ends[0:4]
        rim_high = rim.astype(BF16).astype(F32)
        ends[0:4] = rim_high
        ends[4:8] = rim_high
        ends[8:12] = rim - rim_high
        high, low = halves(block[pl.ds(c * chunk, chunk)])
        both = dot(paired(high, low), rad_main_v[...])
        outside = lax.dot_general(
            ends[...].astype(BF16), rad_use_v[...], (((0,), (0,)), ((), ())),
            preferred_element_type=F32,
        )
        slope = (both[:, :cells_r] + both[:, cells_r:] + outside) * metric[...]
        grad_radial[pl.ds(c * chunk, chunk)] = slope.reshape(chunk, cells_t, cells_r)

    for copy in azimuth_copies:
        copy.wait()


def stacked(high, low, p):
    return jnp.concatenate(
        [jnp.concatenate([high[q], high[q], low[q]], axis=0) for q in (p, p + 1)], axis=1
    )


def paired(high, low):
    planes, cells_t, cells_r = high.shape
    rows = planes * cells_t
    return jnp.concatenate([high.reshape(rows, cells_r), low.reshape(rows, cells_r)], axis=1)


def join_kernel(
    chunk, part_slope, part_smooth, radial, from_left, from_right, azi_use, azimuth_metric,
    grad_azimuth, filtered, grad_radial,
    slopes, smooths, rims, radial_sem, sems,
):
    planes, cells_t, cells_r = part_slope.shape
    count = planes // chunk
    groups = chunk // PACK
    radial_copy = pltpu.make_async_copy(radial, grad_radial, radial_sem)
    radial_copy.start()
    rims[...] = jnp.zeros_like(rims)

    def stores(c):
        span = pl.ds(c * chunk, chunk)
        return [
            pltpu.make_async_copy(source.at[span], target.at[span], sems.at[k, c])
            for k, (source, target) in enumerate(((slopes, grad_azimuth), (smooths, filtered)))
        ]

    @pl.loop(0, count)
    def _(c):
        for p in range(chunk):
            group, slot = divmod(p, PACK)
            span = slice(EDGE * slot, EDGE * (slot + 1))
            rims[p, 0:EDGE, :] = from_left[c * groups + group, span, :]
            rims[p, 8 : 8 + EDGE, :] = from_right[c * groups + group, span, :]
        high, low = halves(rims[...])
        for p in range(0, chunk, 2):
            result = dot(azi_use[...], stacked(high, low, p))
            for k in range(2):
                q = c * chunk + p + k
                lanes = slice(k * cells_r, (k + 1) * cells_r)
                slopes[q] = (part_slope[q] + result[:cells_t, lanes]) * azimuth_metric[...]
                smooths[q] = part_smooth[q] + result[cells_t:, lanes]
        for copy in stores(c):
            copy.start()

    @pl.loop(0, count)
    def _(c):
        for copy in stores(c):
            copy.wait()

    radial_copy.wait()


def local(tables, azi_count, rad_count, fields, radial_metric, azimuth_metric):
    azi_send, azi_main, azi_use, rad_send, rad_main, rad_use = [jnp.asarray(t) for t in tables]
    shape = fields.shape
    cells_t, cells_r = shape[2], shape[3]
    planes = shape[0] * shape[1]
    x = fields.reshape(planes, cells_t, cells_r)
    chunk = 8
    count = planes // chunk
    rims = jax.ShapeDtypeStruct((planes // PACK, PACK * EDGE, cells_r), F32)
    full = jax.ShapeDtypeStruct(x.shape, F32)
    ends = pltpu.VMEM((2, planes * cells_t), F32)
    hbm = pl.BlockSpec(memory_space=pltpu.HBM)
    vmem = pl.BlockSpec(memory_space=pltpu.VMEM)
    dma = pltpu.SemaphoreType.DMA
    from_left, from_right, part_slope, part_smooth, radial = pl.pallas_call(
        functools.partial(block_kernel, azi_count, rad_count, chunk),
        out_shape=[rims, rims, full, full, full],
        in_specs=[hbm] * 7,
        out_specs=[vmem] * 5,
        scratch_shapes=[
            pltpu.VMEM(x.shape, F32),
            pltpu.VMEM(azi_send.shape, BF16),
            pltpu.VMEM(azi_main.shape, BF16),
            pltpu.VMEM(rad_send.shape[1:], BF16),
            pltpu.VMEM(rad_main.shape[1:], BF16),
            pltpu.VMEM(rad_use.shape[1:], BF16),
            pltpu.VMEM((1, cells_r), F32),
            pltpu.VMEM(rims.shape, F32),
            pltpu.VMEM(rims.shape, F32),
            ends,
            ends,
            ends,
            ends,
            pltpu.VMEM((16, chunk * cells_t), F32),
            dma((6,)),
            dma((count,)),
            dma((2, 1)),
            dma((2, 1)),
            dma((2,)),
            dma((2,)),
        ],
        compiler_params=pltpu.CompilerParams(
            collective_id=0, has_side_effects=True, vmem_limit_bytes=24 * 2**20
        ),
    )(
        *[
            pltpu.with_memory_space_constraint(a, pltpu.HBM)
            for a in (x, azi_send, azi_main, rad_send, rad_main, rad_use, radial_metric.reshape(1, cells_r))
        ]
    )

    outs = pl.pallas_call(
        functools.partial(join_kernel, chunk),
        out_shape=[full] * 3,
        in_specs=[vmem] * 7,
        out_specs=[hbm] * 3,
        scratch_shapes=[
            pltpu.VMEM(x.shape, F32),
            pltpu.VMEM(x.shape, F32),
            pltpu.VMEM((chunk, 16, cells_r), F32),
            dma,
            dma((2, count)),
        ],
        compiler_params=pltpu.CompilerParams(vmem_limit_bytes=24 * 2**20),
    )(
        part_slope, part_smooth, radial, from_left, from_right, azi_use,
        azimuth_metric.reshape(1, cells_r),
    )
    grad_azimuth, filtered, grad_radial = [a.reshape(shape) for a in outs]
    return grad_azimuth, grad_radial, filtered


def solution(mesh):
    rad_count, azi_count = mesh.shape["rad"], mesh.shape["azi"]
    spec = P(None, None, "azi", "rad")

    def run(fields, radial_metric, azimuth_metric):
        tables = build_tables(
            fields.shape[2] // azi_count, azi_count, fields.shape[3] // rad_count, rad_count
        )
        body = functools.partial(local, tables, azi_count, rad_count)
        return jax.shard_map(
            body,
            mesh=mesh,
            in_specs=(spec, P("rad"), P("rad")),
            out_specs=(spec, spec, spec),
            check_vma=False,
        )(fields, radial_metric, azimuth_metric)

    return run
```
